512 devices in a mesh: ctx: 32 (over y, x, core), exp: 16 (over z).
Axes of the slice: x: 4, y: 4, z: 16, core: 2. Of those that a mesh axis runs over, the one named last changes fastest.
Arguments:
- queries: bfloat16 [2048, 64, 576], P('ctx', 'exp'), may hold values from -5 to 5
- out_grad: bfloat16 [2048, 64, 512], P('ctx', 'exp'), may hold values from -3 to 3
- attn_out: bfloat16 [2048, 64, 512], P('ctx', 'exp'), may hold values from -5 to 5
- log_totals: bfloat16 [64, 2048], P('exp', 'ctx')
- latents: bfloat16 [2048, 576], P('ctx'), may hold values from -5 to 5
- moe_inputs: bfloat16 [2048, 7168], P('exp', 'ctx'), may hold values from -6 to 6
- moe_grad: bfloat16 [2048, 7168], P('exp', 'ctx'), may hold values from -6 to 6
- expert_ids: int32 [2048, 1], P('exp'), may hold values from 0 to 15; in each aligned block of 128 rows (0 to 127, 128 to 255, ...) at most 16 rows name the same one
- gate_weight: bfloat16 [16, 7168, 1024], P('exp', 'ctx'), may hold values from -0.0625 to 0.0625
- up_weight: bfloat16 [16, 7168, 1024], P('exp', 'ctx'), may hold values from -0.0625 to 0.0625
- down_weight: bfloat16 [16, 7168, 1024], P('exp', 'ctx'), may hold values from -0.0625 to 0.0625
Outputs:
- query_grad: bfloat16 [2048, 64, 576], P('ctx', 'exp')
- latent_grad: bfloat16 [2048, 576], P('ctx')
- input_grad: bfloat16 [2048, 7168], P('exp', 'ctx')
- gate_grad: bfloat16 [16, 7168, 1024], P('exp', 'ctx')
- up_grad: bfloat16 [16, 7168, 1024], P('exp', 'ctx')
- down_grad: bfloat16 [16, 7168, 1024], P('exp', 'ctx')
The draws below stay inside these ranges and needn't reach their ends.
Inputs may be any that keep to these rules, and one draw needn't show every extreme that they name: `expert_ids`: among the 128 rows of one index of exp no expert is named by more than 16 rows; in some such block one expert is named by exactly 16.
All inputs are finite; a program needn't handle non-finite values.
Results may differ from the reference program's by a relative error of at most 0.0053.
Values may be sent and summed in bfloat16 or wider, within the bound.
A program may use at most 128 MiB of HBM per device.

```python
import math
import jax
import jax.numpy as jnp
import numpy as np
from jax import lax

SEQ = 2048
H = 64
L = 512
R = 64
KV = 576
D = 7168
F = 1024
EXPERTS = 16
TOK_E = 128
ROWS = 2048
BLK = 16
N_EXP = 16


def draw_log_totals(key, part):
    key = jax.random.fold_in(key, 7)
    base = jnp.log(jnp.arange(SEQ, dtype=jnp.float32) + 1.0) + 1.5
    noise = jax.random.uniform(key, (H, SEQ), jnp.float32, -0.5, 0.5)
    return (base[None, :] + noise).astype(jnp.bfloat16)


def level_of(key, extent, shards, smallest, top_value):
    factor_of = 1.0
    for axis_at, parts in shards:
        heights = jax.random.uniform(jax.random.fold_in(jax.random.fold_in(key, 6), axis_at), (parts,), jnp.float32, smallest / len(shards), top_value / len(shards))
        factor_of = factor_of * jnp.repeat(jnp.exp(heights), extent[axis_at] // parts).reshape((-1,) + (1,) * (len(extent) - 1 - axis_at))
    return factor_of


def shared_out(key, own, number, rows, number_of, top, bound, lean):
    sequence = jax.random.permutation(key, number_of)
    heavy_load, common = load_shares(number_of, rows * top, bound, lean, True), load_shares(number_of, rows * top, bound, lean, False)
    places = jnp.arange(number_of)

    def named(tallies, turn):
        used = int((tallies > 0).sum())
        fixed = max(1, used // 4)
        shifted = fixed + (places - fixed + turn * (used - fixed)) % max(1, number_of - fixed)
        return jnp.zeros((number_of,), jnp.int32).at[sequence[jnp.where(places < fixed, places, shifted)]].set(jnp.asarray(tallies, jnp.int32))

    tallies = jnp.where(number % 4 == 0, named(heavy_load, number // 4), named(common, number - number // 4 - 1))
    mixed = jax.random.permutation(jax.random.fold_in(own, 3), number_of)
    donor, taker = mixed[0:number_of // 2 * 2:2], mixed[1:number_of // 2 * 2:2]
    slack = jnp.minimum(tallies[donor] - 1, bound - tallies[taker]) // 2
    slack = jnp.where((donor == sequence[0]) | (taker == sequence[0]) | (tallies[taker] == 0), 0, jnp.maximum(slack, 0))
    shifted = jax.random.randint(jax.random.fold_in(own, 4), (number_of // 2,), 0, 1 << 20) % (slack + 1)
    tallies = tallies.at[donor].add(-shifted).at[taker].add(shifted)
    members = jnp.searchsorted(jnp.cumsum(tallies), jnp.arange(rows * top), side="right").astype(jnp.int32)
    grid = members.reshape(top, rows).T
    grid = grid[jax.random.permutation(jax.random.fold_in(own, 1), rows)]
    turn = jax.random.randint(jax.random.fold_in(own, 2), (rows, 1), 0, top)
    return jnp.take_along_axis(grid, (jnp.arange(top)[None, :] + turn) % top, axis=1)


def load_shares(count, total, reach, skew, full):
    weights = [(1 << 20) // math.isqrt(rank ** skew) + 1 for rank in range(1, count + 1)]
    largest = reach if full else min(reach, max(-(-total // count), total * weights[0] // sum(weights)))
    least = 1 if total - largest >= count - 1 else 0
    counts, rest = [largest] + [least] * (count - 1), total - largest - least * (count - 1)
    while rest > 0:
        movable = [i for i in range(1, count) if counts[i] < largest] or [i for i in range(1, count) if counts[i] < reach]
        whole, remaining = sum([weights[i] for i in movable]), rest
        for i in movable:
            extra = min(reach - counts[i], max(1, remaining * weights[i] // whole), rest)
            counts[i] = counts[i] + extra
            rest = rest - extra
    return np.array(counts)


def centred(own_key, extent, deviation, limit, cuts=(), kind=jnp.bfloat16):
    result = deviation * jax.random.normal(own_key, extent, jnp.float32)
    if cuts:
        result = result * level_of(own_key, extent, cuts, -0.22, 0.18)
    return jnp.clip(result, -limit, limit).astype(kind)


def setup_inputs(seed: int = 0) -> dict:
    key_list = jax.random.split(jax.random.key(seed), 12)
    queries = centred(key_list[0], (SEQ, H, KV), 1.0, 5.0, ((0, 32), (1, 16)))
    out_grad = centred(key_list[1], (SEQ, H, L), 0.5, 3.0, ((0, 32), (1, 16)))
    attn_out = centred(key_list[2], (SEQ, H, L), 1.0, 5.0, ((0, 32), (1, 16)))
    log_totals = draw_log_totals(jax.random.fold_in(key_list[11], 71), 0)
    latents = centred(key_list[4], (SEQ, KV), 1.0, 5.0, ((0, 32),))
    moe_inputs = centred(key_list[5], (ROWS, D), 1.0, 6.0, ((0, 16), (1, 32)))
    moe_grad = centred(key_list[6], (ROWS, D), 1.0, 6.0, ((0, 16), (1, 32)))
    expert_ids_keys = jax.random.split(jax.random.fold_in(key_list[7], 1), ROWS // TOK_E)
    expert_ids_turns = jax.random.permutation(jax.random.fold_in(key_list[7], 3), ROWS // TOK_E)
    expert_ids = jax.vmap(lambda own, number: shared_out(jax.random.fold_in(key_list[7], 2), own, number, TOK_E, EXPERTS, 1, BLK, 2))(expert_ids_keys, expert_ids_turns).reshape((ROWS, 1))
    gate_weight = centred(key_list[8], (EXPERTS, D, F), D ** -0.5, 0.0625, ((0, 16), (1, 32)))
    up_weight = centred(key_list[9], (EXPERTS, D, F), D ** -0.5, 0.0625, ((0, 16), (1, 32)))
    down_weight = centred(key_list[10], (EXPERTS, D, F), D ** -0.5, 0.0625, ((0, 16), (1, 32)))
    return dict(queries=queries, out_grad=out_grad, attn_out=attn_out, log_totals=log_totals, latents=latents, moe_inputs=moe_inputs, moe_grad=moe_grad, expert_ids=expert_ids, gate_weight=gate_weight, up_weight=up_weight, down_weight=down_weight)


score_scale = 192.0 ** -0.5


def attention_backward(queries, out_grad, attn_out, log_totals, latents):
    seq = queries.shape[0]
    positions = jnp.arange(seq, dtype=jnp.int32)
    causal = positions[None, :] <= positions[:, None]
    values = latents[:, :L]

    def per_head(total, inputs):
        query, grad, output, logs = inputs
        delta = jnp.sum(grad.astype(jnp.float32) * output.astype(jnp.float32), axis=1)
        delta = lax.optimization_barrier(delta.astype(jnp.bfloat16)).astype(jnp.float32)
        logs_wide = logs.astype(jnp.float32)
        scores = jnp.dot(query, latents.T, preferred_element_type=jnp.float32) * score_scale
        weights = jnp.where(causal, jnp.exp(scores - logs_wide[:, None]), jnp.float32(0.0))
        dweights = jnp.dot(grad, values.T, preferred_element_type=jnp.float32)
        dscores = weights * (dweights - delta[:, None])
        weights_b = weights.astype(jnp.bfloat16)
        dscores_b = dscores.astype(jnp.bfloat16)
        query_part = (jnp.dot(dscores_b, latents, preferred_element_type=jnp.float32) * score_scale).astype(jnp.bfloat16)
        key_part = jnp.dot(dscores_b.T, query, preferred_element_type=jnp.float32) * score_scale
        value_part = jnp.dot(weights_b.T, grad, preferred_element_type=jnp.float32)
        total = total + key_part + jnp.pad(value_part, ((0, 0), (0, R)))
        return total, query_part

    start = jnp.zeros(latents.shape, jnp.float32)
    inputs = (jnp.transpose(queries, (1, 0, 2)), jnp.transpose(out_grad, (1, 0, 2)),
              jnp.transpose(attn_out, (1, 0, 2)), log_totals)
    total, query_parts = lax.scan(per_head, start, inputs)
    return jnp.transpose(query_parts, (1, 0, 2)), total.astype(jnp.bfloat16)


def expert_step(gate, upper, dhidden):
    sig = jax.nn.sigmoid(gate)
    active = gate * sig
    hidden = (active * upper).astype(jnp.bfloat16)
    gate_delta = (dhidden * upper * sig * (1.0 + gate * (1.0 - sig))).astype(jnp.bfloat16)
    up_delta = (dhidden * active).astype(jnp.bfloat16)
    return hidden, gate_delta, up_delta


def experts_backward(moe_inputs, moe_grad, expert_ids, gate_weight, up_weight, down_weight):
    chosen = expert_ids[:, 0].reshape(N_EXP, TOK_E)
    onehot = (chosen[:, :, None] == jnp.arange(EXPERTS, dtype=jnp.int32)[None, None, :]).astype(jnp.int32)
    earlier = jnp.cumsum(onehot, axis=1) - onehot
    rank = jnp.sum(earlier * onehot, axis=2).astype(jnp.int32)
    group = jnp.broadcast_to(jnp.arange(N_EXP, dtype=jnp.int32)[:, None], (N_EXP, TOK_E))
    empty = jnp.zeros((EXPERTS, N_EXP, BLK, D), moe_inputs.dtype)
    input_buf = empty.at[chosen, group, rank].set(moe_inputs.reshape(N_EXP, TOK_E, D))
    grad_buf = empty.at[chosen, group, rank].set(moe_grad.reshape(N_EXP, TOK_E, D))

    def per_expert(inputs):
        rows_in, rows_grad, w_gate, w_up, w_down = inputs
        rows_in = rows_in.reshape(N_EXP * BLK, D)
        rows_grad = rows_grad.reshape(N_EXP * BLK, D)
        gate = jnp.dot(rows_in, w_gate, preferred_element_type=jnp.float32)
        upper = jnp.dot(rows_in, w_up, preferred_element_type=jnp.float32)
        dhidden = jnp.dot(rows_grad, w_down, preferred_element_type=jnp.float32)
        hidden, gate_delta, up_delta = expert_step(gate, upper, dhidden)
        back = jnp.dot(gate_delta, w_gate.T, preferred_element_type=jnp.float32)
        back = (back + jnp.dot(up_delta, w_up.T, preferred_element_type=jnp.float32)).astype(jnp.bfloat16)
        gate_part = jnp.dot(rows_in.T, gate_delta, preferred_element_type=jnp.float32).astype(jnp.bfloat16)
        up_part = jnp.dot(rows_in.T, up_delta, preferred_element_type=jnp.float32).astype(jnp.bfloat16)
        down_part = jnp.dot(rows_grad.T, hidden, preferred_element_type=jnp.float32).astype(jnp.bfloat16)
        return back.reshape(N_EXP, BLK, D), gate_part, up_part, down_part

    back_buf, gate_grad, up_grad, down_grad = lax.map(
        per_expert, (input_buf, grad_buf, gate_weight, up_weight, down_weight))
    input_grad = back_buf[chosen, group, rank].reshape(N_EXP * TOK_E, D)
    return input_grad, gate_grad, up_grad, down_grad


def reference(queries, out_grad, attn_out, log_totals, latents, moe_inputs, moe_grad, expert_ids, gate_weight, up_weight, down_weight):
    query_grad, latent_grad = attention_backward(queries, out_grad, attn_out, log_totals, latents)
    input_grad, gate_grad, up_grad, down_grad = experts_backward(
        moe_inputs, moe_grad, expert_ids, gate_weight, up_weight, down_weight)
    return (query_grad, latent_grad, input_grad, gate_grad, up_grad, down_grad)
```

```python
import functools
import math

import jax
import jax.numpy as jnp
from jax import lax
from jax.experimental import pallas as pl
from jax.experimental.pallas import tpu as pltpu
from jax.sharding import PartitionSpec as P

MESH = pl.DeviceIdType.MESH
score_scale = 192.0 ** (-0.5)
BF = jnp.bfloat16
F32 = jnp.float32

K_LAT, K_LATF, K_TOK, K_PAIR, K_SUM, K_DEL, K_DELF, K_BACK, K_KPAIR, K_KSUM, K_ZSUM, K_ZOUT = range(12)
KINDS = 12
L_Q, L_G, L_A, L_WG, L_WU, L_WD = range(6)


def nn(a, b):
    return jnp.dot(a, b, preferred_element_type=F32)


def nt(a, b):
    return lax.dot_general(a, b, (((1,), (1,)), ((), ())), preferred_element_type=F32)


def tn(a, b):
    return lax.dot_general(a, b, (((0,), (0,)), ((), ())), preferred_element_type=F32)


def expert_step(gate, upper, dhidden):
    sig = jax.nn.sigmoid(gate)
    active = gate * sig
    hidden = (active * upper).astype(BF)
    gate_delta = (dhidden * upper * sig * (1.0 + gate * (1.0 - sig))).astype(BF)
    up_delta = (dhidden * active).astype(BF)
    return hidden, gate_delta, up_delta


def body(
    chips,
    side,
    groups,
    q_in,
    g_in,
    a_in,
    log_in,
    lat_in,
    x_in,
    xg_in,
    ids_in,
    wg_in,
    wu_in,
    wd_in,
    qg_out,
    lg_out,
    ig_out,
    gg_out,
    ug_out,
    dg_out,
    q3,
    g3,
    a3,
    wg,
    wu,
    wd,
    q_ref,
    g_ref,
    logs_row,
    delta_row,
    place,
    obuf,
    arr,
    pair_out,
    pair_in,
    own,
    sum_out,
    sum_in,
    dl,
    back_out,
    ret,
    lat_all,
    qacc,
    kp,
    kp_b,
    kpair_in,
    ksum_out,
    ksum_in,
    zpart,
    zsum_in,
    zfin,
    zout,
    send_sem,
    recv_sem,
    local_sem,
):
    c = lax.axis_index("ctx")
    z = lax.axis_index("exp")
    chip = c // 2
    core = c % 2
    sib = (chip * 2 + (1 - core), z)
    length = lat_in.shape[0]
    heads = q_in.shape[1]
    rows = length * heads
    width = x_in.shape[0]
    latent = g_in.shape[2]
    full = lat_in.shape[1]
    half = wg_in.shape[1] // 2
    blk = 16
    tokens = x_in.shape[1]
    owners = min(4, groups)
    spacing = groups // owners
    share = length // owners

    def plane(s):
        y = (chip // side + s // side) % side
        x = (chip % side + s % side) % side
        return y * side + x

    def plane_back(s):
        y = (chip // side + side - s // side) % side
        x = (chip % side + side - s % side) % side
        return y * side + x

    def to(src, dst, kind, si, ri, dev):
        return pltpu.make_async_remote_copy(
            src_ref=src,
            dst_ref=dst,
            send_sem=send_sem.at[kind, si],
            recv_sem=recv_sem.at[kind, ri],
            device_id=dev,
            device_id_type=MESH,
        )

    def arrived(dst, kind, ri):
        to(dst, dst, kind, 0, ri, sib).wait_recv()

    def sent(src, kind, si):
        to(src, src, kind, si, 0, sib).wait_send()

    def each(lo, hi, f):
        def step(i, carry):
            f(i)
            return carry

        lax.fori_loop(lo, hi, step, 0)

    def peer(q):
        return (2 * q + core, z)

    def fetch(src, dst, i):
        return pltpu.make_async_copy(src, dst, local_sem.at[i])

    loads = [
        fetch(wg_in, wg, L_WG),
        fetch(wu_in, wu, L_WU),
        fetch(wd_in, wd, L_WD),
        fetch(q_in, q3, L_Q),
        fetch(g_in, g3, L_G),
        fetch(a_in, a3, L_A),
    ]
    for load in loads:
        load.start()

    chunk = min(256, lat_all.shape[0])
    per = chunk // length
    last = c // per
    lat_all[pl.ds(pl.multiple_of(last * chunk, chunk), chunk), :] = jnp.zeros((chunk, full), BF)
    my_rows = pl.ds(pl.multiple_of(c * length, length), length)
    lat_all[my_rows, :] = lat_in[...]

    barrier = pltpu.get_barrier_semaphore()

    def greet_plane(s):
        pl.semaphore_signal(barrier, inc=1, device_id=peer(plane(s)), device_id_type=MESH)

    def greet_line(s):
        pl.semaphore_signal(barrier, inc=1, device_id=(c, (z + s) % groups), device_id_type=MESH)

    each(1, groups, greet_line)
    each(1, chips, greet_plane)
    pl.semaphore_signal(barrier, inc=1, device_id=sib, device_id_type=MESH)

    chosen = ids_in[...]
    experts = groups
    onehot = (lax.broadcasted_iota(jnp.int32, (experts, tokens), 0) == chosen).astype(F32)
    before = lax.broadcasted_iota(jnp.int32, (tokens, tokens), 0) < lax.broadcasted_iota(
        jnp.int32, (tokens, tokens), 1
    )
    earlier = nn(onehot.astype(BF), before.astype(F32).astype(BF))
    rank = jnp.sum(earlier * onehot, axis=0, keepdims=True)
    slot = chosen * blk + rank.astype(jnp.int32)
    place[...] = (
        (lax.broadcasted_iota(jnp.int32, (experts * blk, tokens), 0) == slot)
        .astype(F32)
        .astype(BF)
    )
    obuf[0] = nt(place[...], x_in[...]).astype(BF)
    obuf[1] = nt(place[...], xg_in[...]).astype(BF)
    mine = pl.ds(pl.multiple_of(z * blk, blk), blk)
    arr[:, mine, :] = obuf[:, mine, :]

    pl.semaphore_wait(barrier, groups + chips - 1)

    def line_rows(zz):
        return pl.ds(pl.multiple_of(zz * blk, blk), blk)

    def send_tokens(s):
        zz = (z + s) % groups
        to(obuf.at[:, line_rows(zz), :], arr.at[:, mine, :], K_TOK, s, z, (c, zz)).start()

    each(1, groups, send_tokens)

    def send_latents(q):
        to(lat_all.at[my_rows, :], lat_all.at[my_rows, :], K_LAT, q, chip, peer(q)).start()

    each(chip + 1, chips, send_latents)

    @pl.when(core == 0)
    def _():
        to(lat_all.at[my_rows, :], lat_all.at[my_rows, :], K_LATF, chip, chip, sib).start()

    for i in (L_Q, L_G, L_A):
        loads[{L_Q: 3, L_G: 4, L_A: 5}[i]].wait()
    q_ref[...] = q3[...].reshape(rows, full)
    g_ref[...] = g3[...].reshape(rows, latent)
    delta = jnp.sum(
        g_ref[...].astype(F32) * a3[...].reshape(rows, latent).astype(F32), axis=1, keepdims=True
    )
    delta = delta.astype(BF).astype(F32)
    diagonal = lax.broadcasted_iota(jnp.int32, (rows, rows), 0) == lax.broadcasted_iota(
        jnp.int32, (rows, rows), 1
    )
    delta_row[...] = jnp.sum(jnp.where(diagonal, delta, 0.0), axis=0, keepdims=True)
    spread = lax.broadcasted_iota(jnp.int32, (length, rows), 0) == (
        lax.broadcasted_iota(jnp.int32, (length, rows), 1) // heads
    )
    by_head = nn(log_in[...], spread.astype(F32).astype(BF))
    of_head = lax.broadcasted_iota(jnp.int32, (heads, rows), 0) == (
        lax.broadcasted_iota(jnp.int32, (heads, rows), 1) % heads
    )
    logs_row[...] = jnp.sum(jnp.where(of_head, by_head, 0.0), axis=0, keepdims=True)

    for i in range(3):
        loads[i].wait()

    def tokens_here(s):
        zz = (z + groups - s) % groups
        arrived(arr.at[:, line_rows(zz), :], K_TOK, zz)

    each(1, groups, tokens_here)

    other_cols = pl.ds(pl.multiple_of((1 - core) * half, half), half)
    my_cols = pl.ds(pl.multiple_of(core * half, half), half)
    for j, (w, side_of) in enumerate(((wg, 0), (wu, 0), (wd, 1))):
        pair_out[j] = nn(arr[side_of], w[:, other_cols])
        to(pair_out.at[j], pair_in.at[j], K_PAIR, j, j, sib).start()
    for j, (w, side_of) in enumerate(((wg, 0), (wu, 0), (wd, 1))):
        own[j] = nn(arr[side_of], w[:, my_cols])

    def block_rows(b):
        return pl.ds(pl.multiple_of(b * length, length), length)

    def pass_latents(q):
        here = lat_all.at[block_rows(2 * q + core), :]
        arrived(here, K_LAT, q)
        to(here, here, K_LATF, q, q, sib).start()

    each(0, chip, pass_latents)

    for j in range(3):
        arrived(pair_in.at[j], K_PAIR, j)
        both = own[j] + pair_in[j]
        sum_out[:, j] = both.reshape(chips, blk, half).astype(BF)

    def send_sums(s):
        q = plane(s)
        to(sum_out.at[q], sum_in.at[chip], K_SUM, s, chip, peer(q)).start()

    each(1, chips, send_sums)
    sum_in[chip] = sum_out[chip]

    def latents_here(q):
        arrived(lat_all.at[block_rows(2 * q + 1 - core), :], K_LATF, q)

    each(0, chip + core, latents_here)
    qacc[...] = jnp.zeros_like(qacc)

    def visit(m, carry):
        at = pl.ds(pl.multiple_of(m * chunk, chunk), chunk)
        keys = lat_all[at, :]
        queries = q_ref[...]
        grads = g_ref[...]
        scores = nt(keys, queries) * score_scale
        key_pos = m * chunk + lax.broadcasted_iota(jnp.int32, (chunk, rows), 0)
        query_pos = c * length + lax.broadcasted_iota(jnp.int32, (chunk, rows), 1) // heads
        weights = jnp.where(key_pos <= query_pos, jnp.exp(scores - logs_row[...]), 0.0)
        dweights = nt(keys[:, :latent], grads)
        dscores = (weights * (dweights - delta_row[...])).astype(BF)
        weights = weights.astype(BF)
        key_part = nn(dscores, queries) * score_scale
        value_part = nn(weights, grads)
        kp[at, :latent] = key_part[:, :latent] + value_part
        kp[at, latent:] = key_part[:, latent:]
        kp_b[at, :] = kp[at, :].astype(BF)
        qacc[...] += tn(dscores, keys)
        for i in range(per // 2):
            q = m * (per // 2) + i

            @pl.when(q < chip + core)
            def _():
                theirs = block_rows(2 * q + 1 - core)
                to(kp_b.at[theirs, :], kpair_in.at[q], K_KPAIR, q, q, sib).start()

        return carry

    lax.fori_loop(0, last + 1, visit, 0)
    qg_out[...] = (qacc[...] * score_scale).astype(BF)

    def sums_here(s):
        q = plane_back(s)
        arrived(sum_in.at[q], K_SUM, q)

    each(1, chips, sums_here)

    def total_of(j):
        total = sum_in[0, j].astype(F32)
        for q in range(1, chips):
            total = total + sum_in[q, j].astype(F32)
        return total

    hidden, gate_delta, up_delta = expert_step(total_of(0), total_of(1), total_of(2))
    dl[core, chip, 0] = hidden
    dl[core, chip, 1] = gate_delta
    dl[core, chip, 2] = up_delta

    def send_deltas(s):
        here = dl.at[core, chip]
        to(here, here, K_DEL, s, chip, peer(plane(s))).start()

    each(1, chips, send_deltas)
    to(dl.at[core, chip], dl.at[core, chip], K_DELF, chip, chip, sib).start()

    def add_pair(q):
        arrived(kpair_in.at[q], K_KPAIR, q)
        both = kp[block_rows(2 * q + core), :] + kpair_in[q].astype(F32)
        ksum_out[q] = both.astype(BF)
        to(ksum_out.at[q], ksum_in.at[chip], K_KSUM, q, chip, peer(q)).start()

    each(0, chip, add_pair)

    @pl.when(core == 0)
    def _():
        arrived(kpair_in.at[chip], K_KPAIR, chip)
        zpart[...] = kp[my_rows, :] + kpair_in[chip].astype(F32)

    @pl.when(core == 1)
    def _():
        zpart[...] = kp[my_rows, :]

    def pass_deltas(s):
        q = plane_back(s)
        here = dl.at[core, q]
        arrived(here, K_DEL, q)
        to(here, here, K_DELF, q, q, sib).start()

    each(1, chips, pass_deltas)

    def deltas_here(q):
        arrived(dl.at[1 - core, q], K_DELF, q)

    each(0, chips, deltas_here)

    def delta_of(h, j):
        return dl[h, :, j].reshape(chips * blk, half)

    back = jnp.zeros((groups * blk, width), F32)
    for h in range(2):
        cols = slice(h * half, (h + 1) * half)
        back = back + nt(delta_of(h, 1), wg[:, cols]) + nt(delta_of(h, 2), wu[:, cols])
    back_out[...] = back.astype(BF)

    def send_back(s):
        zz = (z + s) % groups
        to(back_out.at[line_rows(zz), :], ret.at[mine, :], K_BACK, s, z, (c, zz)).start()

    each(1, groups, send_back)
    ret[mine, :] = back_out[mine, :]

    def add_sum(q):
        arrived(ksum_in.at[q], K_KSUM, q)
        zpart[...] += ksum_in[q].astype(F32)

    each(chip + 1, chips, add_sum)
    zfin[...] = zpart[...].astype(BF)

    def share_rows(i):
        return pl.ds(pl.multiple_of(i * share, share), share)

    def owner_z(i):
        return i * spacing + (spacing // 2) * core

    def send_share(i):
        @pl.when(owner_z(i) != z)
        def _():
            to(
                zfin.at[share_rows(i), :], zsum_in.at[z], K_ZSUM, i, z, (c, owner_z(i))
            ).start()

    each(0, owners, send_share)

    for h in range(2):
        cols = slice(h * half, (h + 1) * half)
        gg_out[:, cols] = tn(arr[0], delta_of(h, 1)).astype(BF)
        ug_out[:, cols] = tn(arr[0], delta_of(h, 2)).astype(BF)
        dg_out[:, cols] = tn(arr[1], delta_of(h, 0)).astype(BF)

    mine_share = z // spacing
    is_owner = owner_z(mine_share) == z

    @pl.when(is_owner)
    def _():
        def shares_here(s):
            zz = (z + s) % groups
            arrived(zsum_in.at[zz], K_ZSUM, zz)

        each(1, groups, shares_here)
        zsum_in[z] = zfin[share_rows(mine_share), :]
        total = zsum_in[0].astype(F32)
        for zz in range(1, groups):
            total = total + zsum_in[zz].astype(F32)
        zout[share_rows(mine_share), :] = total.astype(BF)

        def send_rows(s):
            zz = (z + s) % groups
            there = zout.at[share_rows(mine_share), :]
            to(there, there, K_ZOUT, s, mine_share, (c, zz)).start()

        each(1, groups, send_rows)

    def back_here(s):
        zz = (z + groups - s) % groups
        arrived(ret.at[line_rows(zz), :], K_BACK, zz)

    each(1, groups, back_here)
    ig_out[...] = tn(ret[...], place[...]).astype(BF)

    def rows_here(i):
        @pl.when(owner_z(i) != z)
        def _():
            arrived(zout.at[share_rows(i), :], K_ZOUT, i)

    each(0, owners, rows_here)
    lg_out[...] = zout[...]

    one_block = lat_all.at[my_rows, :]
    each(chip + 1, chips, lambda q: sent(one_block, K_LAT, q))
    each(0, chip, lambda q: sent(one_block, K_LATF, q))

    @pl.when(core == 0)
    def _():
        sent(one_block, K_LATF, chip)

    each(1, groups, lambda s: sent(obuf.at[:, mine, :], K_TOK, s))
    for j in range(3):
        sent(pair_out.at[j], K_PAIR, j)
    each(1, chips, lambda s: sent(sum_out.at[0], K_SUM, s))
    each(1, chips, lambda s: sent(dl.at[0, 0], K_DEL, s))
    each(0, chips, lambda q: sent(dl.at[0, 0], K_DELF, q))
    each(0, chip + core, lambda q: sent(ksum_out.at[0], K_KPAIR, q))
    each(0, chip, lambda q: sent(ksum_out.at[0], K_KSUM, q))
    each(1, groups, lambda s: sent(back_out.at[mine, :], K_BACK, s))

    def share_sent(i):
        @pl.when(owner_z(i) != z)
        def _():
            sent(zfin.at[share_rows(0), :], K_ZSUM, i)

    each(0, owners, share_sent)

    @pl.when(is_owner)
    def _():
        each(1, groups, lambda s: sent(zfin.at[share_rows(0), :], K_ZOUT, s))


def shards(
    chips,
    groups,
    queries,
    out_grad,
    attn_out,
    log_totals,
    latents,
    moe_inputs,
    moe_grad,
    expert_ids,
    gate_weight,
    up_weight,
    down_weight,
):
    length, heads, full = queries.shape
    latent = out_grad.shape[2]
    rows = length * heads
    tokens, width = moe_inputs.shape
    hidden = gate_weight.shape[2]
    half = hidden // 2
    blk = 16
    slots = groups * blk
    keys = length * chips * 2
    side = math.isqrt(chips)
    vmem = pl.BlockSpec(memory_space=pltpu.VMEM)
    hbm = pl.BlockSpec(memory_space=pl.ANY)
    lanes = max(chips, groups)
    owners = min(4, groups)
    weight = (width, hidden)
    qg, lg, ig, gg, ug, dg = pl.pallas_call(
        functools.partial(body, chips, side, groups),
        out_shape=(
            jax.ShapeDtypeStruct((rows, full), BF),
            jax.ShapeDtypeStruct((length, full), BF),
            jax.ShapeDtypeStruct((width, tokens), BF),
            jax.ShapeDtypeStruct(weight, BF),
            jax.ShapeDtypeStruct(weight, BF),
            jax.ShapeDtypeStruct(weight, BF),
        ),
        in_specs=[hbm, hbm, hbm, vmem, vmem, vmem, vmem, vmem, hbm, hbm, hbm],
        out_specs=(vmem,) * 6,
        scratch_shapes=[
            pltpu.VMEM((length, heads, full), BF),
            pltpu.VMEM((length, heads, latent), BF),
            pltpu.VMEM((length, heads, latent), BF),
            pltpu.VMEM(weight, BF),
            pltpu.VMEM(weight, BF),
            pltpu.VMEM(weight, BF),
            pltpu.VMEM((rows, full), BF),
            pltpu.VMEM((rows, latent), BF),
            pltpu.VMEM((1, rows), F32),
            pltpu.VMEM((1, rows), F32),
            pltpu.VMEM((slots, tokens), BF),
            pltpu.VMEM((2, slots, width), BF),
            pltpu.VMEM((2, slots, width), BF),
            pltpu.VMEM((3, slots, half), F32),
            pltpu.VMEM((3, slots, half), F32),
            pltpu.VMEM((3, slots, half), F32),
            pltpu.VMEM((chips, 3, blk, half), BF),
            pltpu.VMEM((chips, 3, blk, half), BF),
            pltpu.VMEM((2, chips, 3, blk, half), BF),
            pltpu.VMEM((slots, width), BF),
            pltpu.VMEM((slots, width), BF),
            pltpu.VMEM((keys, full), BF),
            pltpu.VMEM((rows, full), F32),
            pltpu.VMEM((keys, full), F32),
            pltpu.VMEM((keys, full), BF),
            pltpu.VMEM((chips, length, full), BF),
            pltpu.VMEM((chips, length, full), BF),
            pltpu.VMEM((chips, length, full), BF),
            pltpu.VMEM((length, full), F32),
            pltpu.VMEM((groups, length // owners, full), BF),
            pltpu.VMEM((length, full), BF),
            pltpu.VMEM((length, full), BF),
            pltpu.SemaphoreType.DMA((KINDS, lanes)),
            pltpu.SemaphoreType.DMA((KINDS, lanes)),
            pltpu.SemaphoreType.DMA((6,)),
        ],
        compiler_params=pltpu.CompilerParams(
            collective_id=0, has_side_effects=True, vmem_limit_bytes=52 * 1024 * 1024
        ),
    )(
        queries,
        out_grad,
        attn_out,
        log_totals,
        latents,
        jnp.transpose(moe_inputs),
        jnp.transpose(moe_grad),
        expert_ids.reshape(1, tokens),
        gate_weight.reshape(weight),
        up_weight.reshape(weight),
        down_weight.reshape(weight),
    )
    return (
        qg.reshape(length, heads, full),
        lg,
        jnp.transpose(ig),
        gg.reshape((1,) + weight),
        ug.reshape((1,) + weight),
        dg.reshape((1,) + weight),
    )


def solution(mesh):
    chips = mesh.shape["ctx"] // 2
    groups = mesh.shape["exp"]
    return jax.shard_map(
        functools.partial(shards, chips, groups),
        mesh=mesh,
        in_specs=(
            P("ctx", "exp", None),
            P("ctx", "exp", None),
            P("ctx", "exp", None),
            P("exp", "ctx"),
            P("ctx", None),
            P("exp", "ctx"),
            P("exp", "ctx"),
            P("exp", None),
            P("exp", "ctx", None),
            P("exp", "ctx", None),
            P("exp", "ctx", None),
        ),
        out_specs=(
            P("ctx", "exp", None),
            P("ctx", None),
            P("exp", "ctx"),
            P("exp", "ctx", None),
            P("exp", "ctx", None),
            P("exp", "ctx", None),
        ),
        check_vma=False,
    )
```

```python
import functools
import math

import jax
import jax.numpy as jnp
from jax import lax
from jax.experimental import pallas as pl
from jax.experimental.pallas import tpu as pltpu
from jax.sharding import PartitionSpec as P

MESH = pl.DeviceIdType.MESH
VMEM = 63 * 1024 * 1024
score_scale = 192.0 ** (-0.5)
BF = jnp.bfloat16
F32 = jnp.float32

(
    K_LAT,
    K_LATF,
    K_TOK,
    K_TOKG,
    K_PAIR,
    K_SUM,
    K_SUMD,
    K_DEL,
    K_DELF,
    K_BACK,
    K_KPAIR,
    K_KSUM,
    K_KCOL,
    K_ZSUM,
    K_ZOUT,
) = range(15)
KINDS = 15
(
    L_LAT,
    L_IDS,
    L_X,
    L_XG,
    L_WG,
    L_WU,
    L_WD,
    L_Q,
    L_G,
    L_A,
    L_LOG,
    O_QG,
    O_LG,
    O_IG,
    O_GG,
    O_UG,
    O_DG,
) = range(17)


def nn(a, b):
    return jnp.dot(a, b, preferred_element_type=F32)


def nt(a, b):
    return lax.dot_general(a, b, (((1,), (1,)), ((), ())), preferred_element_type=F32)


def tn(a, b):
    return lax.dot_general(a, b, (((0,), (0,)), ((), ())), preferred_element_type=F32)


def expert_step(gate, upper, dhidden):
    sig = jax.nn.sigmoid(gate)
    active = gate * sig
    hidden = (active * upper).astype(BF)
    gate_delta = (dhidden * upper * sig * (1.0 + gate * (1.0 - sig))).astype(BF)
    up_delta = (dhidden * active).astype(BF)
    return hidden, gate_delta, up_delta


def body(
    chips,
    side,
    groups,
    q_in,
    g_in,
    a_in,
    log_in,
    lat_in,
    x_in,
    xg_in,
    ids_in,
    wg_in,
    wu_in,
    wd_in,
    qg_out,
    lg_out,
    ig_out,
    gg_out,
    ug_out,
    dg_out,
    q3,
    g3,
    a3,
    logs,
    ids,
    xt,
    xgt,
    wg,
    wu,
    wd,
    q_ref,
    g_ref,
    logs_row,
    delta_row,
    place,
    obuf,
    arr,
    pair_out,
    pair_in,
    own,
    sum_out,
    sum_in,
    dl,
    back_out,
    ret,
    lat_all,
    qacc,
    kp,
    kp_b,
    kpair_in,
    ksum_out,
    ksum_in,
    kcol_out,
    kcol_in,
    zpart,
    zsum_in,
    zfin,
    zout,
    igt,
    lgt,
    lat_own,
    gg,
    ug,
    dg,
    send_sem,
    recv_sem,
    local_sem,
):
    c = lax.axis_index("ctx")
    z = lax.axis_index("exp")
    chip = lax.div(c, 2)
    core = lax.rem(c, 2)
    sib = (chip * 2 + (1 - core), z)
    length, full = lat_in.shape
    heads = q_in.shape[1]
    rows = length * heads
    width, tokens = x_in.shape
    latent = g_in.shape[2]
    half = wg_in.shape[1] // 2
    blk = 16
    experts = groups
    owners = min(4, groups)
    spacing = groups // owners
    share = length // owners
    chunk = min(256, lat_all.shape[0])
    per = chunk // length
    last = lax.div(c, per)
    here_y = lax.div(chip, side)
    here_x = lax.rem(chip, side)

    def plane(s):
        y = lax.rem(here_y + lax.div(s, side), side)
        x = lax.rem(here_x + lax.rem(s, side), side)
        return y * side + x

    def plane_back(s):
        y = lax.rem(here_y + side - lax.div(s, side), side)
        x = lax.rem(here_x + side - lax.rem(s, side), side)
        return y * side + x

    first = here_x * (1 - core) + here_y * core
    second = here_y * (1 - core) + here_x * core

    def at(f, g):
        return (g * side + f) * (1 - core) + (f * side + g) * core

    def turned(v, s):
        return lax.rem(v + s, side)

    def ahead(s):
        return lax.rem(z + s, groups)

    def behind(s):
        return lax.rem(z + groups - s, groups)

    def to(src, dst, kind, si, ri, dev):
        return pltpu.make_async_remote_copy(
            src_ref=src,
            dst_ref=dst,
            send_sem=send_sem.at[kind, si],
            recv_sem=recv_sem.at[kind, ri],
            device_id=dev,
            device_id_type=MESH,
        )

    def arrived(dst, kind, ri):
        to(dst, dst, kind, 0, ri, sib).wait_recv()

    def sent(src, kind, si):
        to(src, src, kind, si, 0, sib).wait_send()

    def each(lo, hi, f):
        def step(i, carry):
            f(i)
            return carry

        lax.fori_loop(lo, hi, step, 0)

    def peer(q):
        return (2 * q + core, z)

    def line_rows(zz):
        return pl.ds(pl.multiple_of(zz * blk, blk), blk)

    def block_rows(b):
        return pl.ds(pl.multiple_of(b * length, length), length)

    def share_rows(i):
        return pl.ds(pl.multiple_of(i * share, share), share)

    def owner_z(i):
        return i * spacing + (spacing // 2) * core

    mine = line_rows(z)
    my_rows = block_rows(c)
    my_block = lat_all.at[my_rows, :]
    mine_share = lax.div(z, spacing)
    is_owner = owner_z(mine_share) == z
    other_cols = pl.ds(pl.multiple_of((1 - core) * half, half), half)
    my_cols = pl.ds(pl.multiple_of(core * half, half), half)
    barrier = pltpu.get_barrier_semaphore()

    def gather_start(block, kind):
        for s in range(1, side):
            to(block(chip), block(chip), kind, s, chip, peer(at(turned(first, s), second))).start()

    def gather_second(block, kind, f):
        held = at(f, second)
        for s in range(1, side):
            si = side * (1 + lax.rem(f - first + side, side)) + s
            to(block(held), block(held), kind, si, held, peer(at(first, turned(second, s)))).start()

    def gather_first_rest(block, kind, fkind):
        def step(s):
            q = at(turned(first, side - s), second)
            arrived(block(q), kind, q)
            gather_second(block, kind, turned(first, side - s))
            to(block(q), block(q), fkind, q, q, sib).start()

        each(1, side, step)

    def gather_second_rest(block, kind, fkind):
        def step(i):
            f = turned(first, side - lax.rem(i, side))
            q = at(f, turned(second, side - lax.div(i, side)))
            arrived(block(q), kind, q)
            to(block(q), block(q), fkind, q, q, sib).start()

        each(side, chips, step)

    def gather_pending(block, kind, fkind):
        pending.append(lambda: each(1, side, lambda s: sent(block, kind, s)))
        pending.append(
            lambda: each(
                0,
                side * (side - 1),
                lambda i: sent(
                    block, kind, side * (1 + lax.div(i, side - 1)) + 1 + lax.rem(i, side - 1)
                ),
            )
        )
        pending.append(lambda: each(0, chips, lambda q: sent(block, fkind, q)))

    def lat_block(q):
        return lat_all.at[block_rows(2 * q + core), :]

    def delta_block(q):
        return dl.at[core, q]

    copies = {}

    def start(src, dst, i):
        copies[i] = pltpu.make_async_copy(src, dst, local_sem.at[i])
        copies[i].start()

    def ready(*which):
        for i in which:
            copies.pop(i).wait()

    pending = []

    def load():
        ksum_out[...] = jnp.zeros_like(ksum_out)
        start(ids_in, ids, L_IDS)
        start(x_in, xt, L_X)
        start(xg_in, xgt, L_XG)
        start(lat_in, lat_own, L_LAT)
        start(wg_in, wg, L_WG)
        start(wu_in, wu, L_WU)
        start(wd_in, wd, L_WD)
        start(q_in, q3, L_Q)
        start(g_in, g3, L_G)
        start(a_in, a3, L_A)
        start(log_in, logs, L_LOG)

    def greet():
        def greet_line(s):
            pl.semaphore_signal(
                barrier, inc=1, device_id=(c, ahead(s)), device_id_type=MESH
            )

        def greet_plane(s):
            pl.semaphore_signal(barrier, inc=1, device_id=peer(plane(s)), device_id_type=MESH)

        each(1, groups, greet_line)
        each(1, chips, greet_plane)
        pl.semaphore_signal(barrier, inc=1, device_id=sib, device_id_type=MESH)

    def dispatch():
        ready(L_IDS, L_X, L_XG)
        chosen = ids[...]
        onehot = (lax.broadcasted_iota(jnp.int32, (experts, tokens), 0) == chosen).astype(F32)
        before = lax.broadcasted_iota(jnp.int32, (tokens, tokens), 0) < lax.broadcasted_iota(
            jnp.int32, (tokens, tokens), 1
        )
        earlier = nn(onehot.astype(BF), before.astype(F32).astype(BF))
        rank = jnp.sum(earlier * onehot, axis=0, keepdims=True)
        slot = chosen * blk + rank.astype(jnp.int32)
        place[...] = (
            (lax.broadcasted_iota(jnp.int32, (experts * blk, tokens), 0) == slot)
            .astype(F32)
            .astype(BF)
        )
        obuf[0, :, :width] = nt(place[...], xt[...]).astype(BF)
        obuf[1, :, :width] = nt(place[...], xgt[...]).astype(BF)
        arr[:, mine, :] = obuf[:, mine, :]

    def met():
        pl.semaphore_wait(barrier, groups + chips - 1)

    def send_tokens_of(part, kind):
        def step(s):
            zz = ahead(s)
            to(obuf.at[part, line_rows(zz), :], arr.at[part, mine, :], kind, s, z, (c, zz)).start()

        each(1, groups, step)
        pending.append(lambda: each(1, groups, lambda s: sent(obuf.at[0, mine, :], kind, s)))

    def send_inputs():
        send_tokens_of(0, K_TOK)

    def send_grads():
        send_tokens_of(1, K_TOKG)

    def send_latents():
        ready(L_LAT)
        lat_all[my_rows, :full] = lat_own[...]
        gather_start(lat_block, K_LAT)
        gather_second(lat_block, K_LAT, first)
        to(my_block, my_block, K_LATF, chip, chip, sib).start()
        gather_pending(my_block, K_LAT, K_LATF)

    def pass_latents():
        gather_first_rest(lat_block, K_LAT, K_LATF)

    def pass_latents_on():
        gather_second_rest(lat_block, K_LAT, K_LATF)

    def row_values():
        ready(L_Q, L_G, L_A, L_LOG)
        q_ref[...] = q3[...].reshape(rows, full)
        g_ref[...] = g3[...].reshape(rows, latent)
        delta = jnp.sum(
            g_ref[...].astype(F32) * a3[...].reshape(rows, latent).astype(F32),
            axis=1,
            keepdims=True,
        )
        delta = delta.astype(BF).astype(F32)
        diagonal = lax.broadcasted_iota(jnp.int32, (rows, rows), 0) == lax.broadcasted_iota(
            jnp.int32, (rows, rows), 1
        )
        delta_row[...] = jnp.sum(jnp.where(diagonal, delta, 0.0), axis=0, keepdims=True)
        spread = lax.broadcasted_iota(jnp.int32, (length, rows), 0) == (
            lax.broadcasted_iota(jnp.int32, (length, rows), 1) // heads
        )
        by_head = nn(logs[...], spread.astype(F32).astype(BF))
        of_head = lax.broadcasted_iota(jnp.int32, (heads, rows), 0) == (
            lax.broadcasted_iota(jnp.int32, (heads, rows), 1) % heads
        )
        logs_row[...] = jnp.sum(jnp.where(of_head, by_head, 0.0), axis=0, keepdims=True)

    def tokens_here_of(part, kind):
        def step(s):
            zz = behind(s)
            arrived(arr.at[part, line_rows(zz), :], kind, zz)

        each(1, groups, step)

    def project_of(j, w, part):
        pair_out[j] = nn(arr[part, :, :width], w[:, other_cols])
        to(pair_out.at[j], pair_in.at[j], K_PAIR, j, j, sib).start()
        pending.append(lambda: sent(pair_out.at[j], K_PAIR, j))

    def project_inputs():
        tokens_here_of(0, K_TOK)
        ready(L_WG, L_WU)
        project_of(0, wg, 0)
        project_of(1, wu, 0)
        own[0] = nn(arr[0, :, :width], wg[:, my_cols])
        own[1] = nn(arr[0, :, :width], wu[:, my_cols])

    def project_grads():
        tokens_here_of(1, K_TOKG)
        ready(L_WD)
        project_of(2, wd, 1)
        own[2] = nn(arr[1, :, :width], wd[:, my_cols])

    def add_pair(j):
        arrived(pair_in.at[j], K_PAIR, j)
        both = own[j] + pair_in[j]
        sum_out[:, j] = both.reshape(chips, blk, half).astype(BF)
        sum_in[chip, j] = sum_out[chip, j]

    def send_sums_of(parts, kind):
        def step(s):
            q = plane(s)
            to(sum_out.at[q, parts], sum_in.at[chip, parts], kind, s, chip, peer(q)).start()

        each(1, chips, step)
        pending.append(lambda: each(1, chips, lambda s: sent(sum_out.at[0, parts], kind, s)))

    def sums_here_of(parts, kind):
        def step(s):
            q = plane_back(s)
            arrived(sum_in.at[q, parts], kind, q)

        each(1, chips, step)

    def send_input_sums():
        add_pair(0)
        add_pair(1)
        send_sums_of(pl.ds(0, 2), K_SUM)

    def send_grad_sums():
        add_pair(2)
        send_sums_of(pl.ds(2, 1), K_SUMD)

    def latents_here():
        each(0, chips, lambda q: arrived(lat_all.at[block_rows(2 * q + 1 - core), :], K_LATF, q))

    def attention():
        qacc[...] = jnp.zeros_like(qacc)

        def visit(m, carry):
            at = pl.ds(pl.multiple_of(m * chunk, chunk), chunk)
            keys = lat_all[at, :full]
            queries = q_ref[...]
            grads = g_ref[...]
            scores = nt(keys, queries) * score_scale
            key_pos = m * chunk + lax.broadcasted_iota(jnp.int32, (chunk, rows), 0)
            query_pos = c * length + lax.broadcasted_iota(jnp.int32, (chunk, rows), 1) // heads
            weights = jnp.where(key_pos <= query_pos, jnp.exp(scores - logs_row[...]), 0.0)
            dweights = nt(keys[:, :latent], grads)
            dscores = (weights * (dweights - delta_row[...])).astype(BF)
            weights = weights.astype(BF)
            key_part = nn(dscores, queries) * score_scale
            value_part = nn(weights, grads)
            kp[at, :latent] = key_part[:, :latent] + value_part
            kp[at, latent:] = key_part[:, latent:]
            kp_b[at, :full] = kp[at, :].astype(BF)
            qacc[...] += tn(dscores, keys)
            for i in range(per // 2):
                q = m * (per // 2) + i

                @pl.when(q < chip + core)
                def _():
                    theirs = block_rows(2 * q + 1 - core)
                    to(kp_b.at[theirs, :], kpair_in.at[q], K_KPAIR, q, q, sib).start()

            return carry

        lax.fori_loop(0, last + 1, visit, 0)
        pending.append(lambda: each(0, chip + core, lambda q: sent(kpair_in.at[0], K_KPAIR, q)))
        q3[...] = (qacc[...] * score_scale).astype(BF).reshape(length, heads, full)
        start(q3, qg_out, O_QG)

    def sums_here():
        sums_here_of(pl.ds(0, 2), K_SUM)
        sums_here_of(pl.ds(2, 1), K_SUMD)

    def experts_step():
        def total_of(j):
            total = sum_in[0, j].astype(F32)
            for q in range(1, chips):
                total = total + sum_in[q, j].astype(F32)
            return total

        hidden, gate_delta, up_delta = expert_step(total_of(0), total_of(1), total_of(2))
        dl[core, chip, 0] = hidden
        dl[core, chip, 1] = gate_delta
        dl[core, chip, 2] = up_delta

    def send_deltas():
        gather_start(delta_block, K_DEL)
        gather_second(delta_block, K_DEL, first)
        here = delta_block(chip)
        to(here, here, K_DELF, chip, chip, sib).start()
        gather_pending(here, K_DEL, K_DELF)

    def key_pairs():
        def step(q):
            arrived(kpair_in.at[q], K_KPAIR, q)
            both = kp[block_rows(2 * q + core), :] + kpair_in[q, :, :full].astype(F32)
            ksum_out[q, :, :full] = both.astype(BF)

        each(0, chip + 1 - core, step)

        @pl.when(core == 1)
        def _():
            ksum_out[chip, :, :full] = kp[my_rows, :].astype(BF)

        def send(i):
            s, g = 1 + lax.div(i, side), lax.rem(i, side)
            f = turned(first, s)
            to(
                ksum_out.at[at(f, g)],
                ksum_in.at[first * side + g],
                K_KSUM,
                i,
                first * side + g,
                peer(at(f, second)),
            ).start()

        each(0, side * (side - 1), send)
        pending.append(
            lambda: each(0, side * (side - 1), lambda i: sent(ksum_out.at[0], K_KSUM, i))
        )

    def key_lines():
        def step(i):
            s, g = 1 + lax.div(i, side), lax.rem(i, side)
            f = turned(first, side - s)
            arrived(ksum_in.at[f * side + g], K_KSUM, f * side + g)

        each(0, side * (side - 1), step)

        def line(g):
            total = ksum_out[at(first, g), :, :full].astype(F32)
            for s in range(1, side):
                total = total + ksum_in[turned(first, s) * side + g, :, :full].astype(F32)
            return total

        def send(s):
            g = turned(second, s)
            kcol_out[s, :, :full] = line(g).astype(BF)
            to(
                kcol_out.at[s], kcol_in.at[second], K_KCOL, s, second, peer(at(first, g))
            ).start()

        each(1, side, send)
        zpart[...] = line(second)
        pending.append(lambda: each(1, side, lambda s: sent(kcol_out.at[0], K_KCOL, s)))

    def pass_deltas():
        gather_first_rest(delta_block, K_DEL, K_DELF)

    def pass_deltas_on():
        gather_second_rest(delta_block, K_DEL, K_DELF)

    def deltas_here():
        each(0, chips, lambda q: arrived(dl.at[1 - core, q], K_DELF, q))

    def delta_of(h, j):
        return dl[h, :, j].reshape(chips * blk, half)

    def go_back():
        back = jnp.zeros((groups * blk, width), F32)
        for h in range(2):
            cols = slice(h * half, (h + 1) * half)
            back = back + nt(delta_of(h, 1), wg[:, cols]) + nt(delta_of(h, 2), wu[:, cols])
        back_out[:, :width] = back.astype(BF)

        def step(s):
            zz = ahead(s)
            to(back_out.at[line_rows(zz), :], ret.at[mine, :], K_BACK, s, z, (c, zz)).start()

        each(1, groups, step)
        ret[mine, :] = back_out[mine, :]
        pending.append(lambda: each(1, groups, lambda s: sent(back_out.at[mine, :], K_BACK, s)))

    def key_sums():
        def step(s):
            g = turned(second, s)
            arrived(kcol_in.at[g], K_KCOL, g)
            zpart[...] += kcol_in[g, :, :full].astype(F32)

        each(1, side, step)
        zfin[:, :full] = zpart[...].astype(BF)

        def send_share(i):
            @pl.when(owner_z(i) != z)
            def _():
                to(
                    zfin.at[share_rows(i), :], zsum_in.at[z], K_ZSUM, i, z, (c, owner_z(i))
                ).start()

        each(0, owners, send_share)

        def share_sent(i):
            @pl.when(owner_z(i) != z)
            def _():
                sent(zfin.at[share_rows(0), :], K_ZSUM, i)

        pending.append(lambda: each(0, owners, share_sent))

    def weight_grads():
        for h in range(2):
            cols = slice(h * half, (h + 1) * half)
            gg[:, cols] = tn(arr[0, :, :width], delta_of(h, 1)).astype(BF)
            ug[:, cols] = tn(arr[0, :, :width], delta_of(h, 2)).astype(BF)
            dg[:, cols] = tn(arr[1, :, :width], delta_of(h, 0)).astype(BF)
        start(gg, gg_out, O_GG)
        start(ug, ug_out, O_UG)
        start(dg, dg_out, O_DG)

    def share_sums():
        @pl.when(is_owner)
        def _():
            def shares_here(s):
                zz = ahead(s)
                arrived(zsum_in.at[zz], K_ZSUM, zz)

            each(1, groups, shares_here)
            zsum_in[z] = zfin[share_rows(mine_share), :]
            total = zsum_in[0, :, :full].astype(F32)
            for zz in range(1, groups):
                total = total + zsum_in[zz, :, :full].astype(F32)
            zout[share_rows(mine_share), :full] = total.astype(BF)

            def send_rows(s):
                zz = ahead(s)
                there = zout.at[share_rows(mine_share), :]
                to(there, there, K_ZOUT, s, mine_share, (c, zz)).start()

            each(1, groups, send_rows)

        def rows_sent():
            @pl.when(is_owner)
            def _():
                each(1, groups, lambda s: sent(zfin.at[share_rows(0), :], K_ZOUT, s))

        pending.append(rows_sent)

    def back_here():
        def step(s):
            zz = behind(s)
            arrived(ret.at[line_rows(zz), :], K_BACK, zz)

        each(1, groups, step)
        igt[...] = tn(ret[:, :width], place[...]).astype(BF)
        start(igt, ig_out, O_IG)

    def rows_here():
        def step(i):
            @pl.when(owner_z(i) != z)
            def _():
                arrived(zout.at[share_rows(i), :], K_ZOUT, i)

        each(0, owners, step)
        lgt[...] = zout[:, :full]
        start(lgt, lg_out, O_LG)

    def finish():
        for wait in pending:
            wait()
        ready(*list(copies))

    for phase in (
        load,
        greet,
        dispatch,
        met,
        send_inputs,
        send_latents,
        send_grads,
        row_values,
        pass_latents,
        pass_latents_on,
        project_inputs,
        send_input_sums,
        latents_here,
        attention,
        project_grads,
        send_grad_sums,
        key_pairs,
        sums_here,
        experts_step,
        send_deltas,
        key_lines,
        pass_deltas,
        key_sums,
        pass_deltas_on,
        deltas_here,
        go_back,
        weight_grads,
        share_sums,
        back_here,
        rows_here,
        finish,
    ):
        phase()


def hand_out(count, *refs):
    stages, sems = refs[2 * count : 3 * count], refs[3 * count]
    ins = [pltpu.make_async_copy(refs[i], stages[i], sems.at[i]) for i in range(count)]
    outs = [
        pltpu.make_async_copy(stages[i], refs[count + i], sems.at[count + i])
        for i in range(count)
    ]
    for copy in ins:
        copy.start()
    for i in range(count):
        ins[i].wait()
        outs[i].start()
    for copy in outs:
        copy.wait()


def shards(
    chips,
    groups,
    queries,
    out_grad,
    attn_out,
    log_totals,
    latents,
    moe_inputs,
    moe_grad,
    expert_ids,
    gate_weight,
    up_weight,
    down_weight,
):
    length, heads, full = queries.shape
    latent = out_grad.shape[2]
    rows = length * heads
    tokens, width = moe_inputs.shape
    hidden = gate_weight.shape[2]
    half = hidden // 2
    blk = 16
    slots = groups * blk
    keys = length * chips * 2
    side = math.isqrt(chips)
    hbm = pl.BlockSpec(memory_space=pltpu.HBM)
    anywhere = pl.BlockSpec(memory_space=pl.ANY)
    lanes = max(chips + side, groups)
    owners = min(4, groups)
    weight = (width, hidden)
    wide = -(-width // 128) * 128
    padded = -(-full // 128) * 128
    results = (
        jax.ShapeDtypeStruct((length, heads, full), BF),
        jax.ShapeDtypeStruct((length, full), BF),
        jax.ShapeDtypeStruct((width, tokens), BF),
        jax.ShapeDtypeStruct(weight, BF),
        jax.ShapeDtypeStruct(weight, BF),
        jax.ShapeDtypeStruct(weight, BF),
    )
    held = pl.pallas_call(
        functools.partial(body, chips, side, groups),
        out_shape=results,
        in_specs=[hbm] * 11,
        out_specs=(anywhere,) * 6,
        scratch_shapes=[
            pltpu.VMEM((length, heads, full), BF),
            pltpu.VMEM((length, heads, latent), BF),
            pltpu.VMEM((length, heads, latent), BF),
            pltpu.VMEM((heads, length), BF),
            pltpu.VMEM((1, tokens), jnp.int32),
            pltpu.VMEM((width, tokens), BF),
            pltpu.VMEM((width, tokens), BF),
            pltpu.VMEM(weight, BF),
            pltpu.VMEM(weight, BF),
            pltpu.VMEM(weight, BF),
            pltpu.VMEM((rows, full), BF),
            pltpu.VMEM((rows, latent), BF),
            pltpu.VMEM((1, rows), F32),
            pltpu.VMEM((1, rows), F32),
            pltpu.VMEM((slots, tokens), BF),
            pltpu.VMEM((2, slots, wide), BF),
            pltpu.VMEM((2, slots, wide), BF),
            pltpu.VMEM((3, slots, half), F32),
            pltpu.VMEM((3, slots, half), F32),
            pltpu.VMEM((3, slots, half), F32),
            pltpu.VMEM((chips, 3, blk, half), BF),
            pltpu.VMEM((chips, 3, blk, half), BF),
            pltpu.VMEM((2, chips, 3, blk, half), BF),
            pltpu.VMEM((slots, wide), BF),
            pltpu.VMEM((slots, wide), BF),
            pltpu.VMEM((keys, padded), BF),
            pltpu.VMEM((rows, full), F32),
            pltpu.VMEM((keys, full), F32),
            pltpu.VMEM((keys, padded), BF),
            pltpu.VMEM((chips, length, padded), BF),
            pltpu.VMEM((chips, length, padded), BF),
            pltpu.VMEM((chips, length, padded), BF),
            pltpu.VMEM((side, length, padded), BF),
            pltpu.VMEM((side, length, padded), BF),
            pltpu.VMEM((length, full), F32),
            pltpu.VMEM((groups, length // owners, padded), BF),
            pltpu.VMEM((length, padded), BF),
            pltpu.VMEM((length, padded), BF),
            pltpu.VMEM((width, tokens), BF),
            pltpu.VMEM((length, full), BF),
            pltpu.VMEM((length, full), BF),
            pltpu.VMEM(weight, BF),
            pltpu.VMEM(weight, BF),
            pltpu.VMEM(weight, BF),
            pltpu.SemaphoreType.DMA((KINDS, lanes)),
            pltpu.SemaphoreType.DMA((KINDS, lanes)),
            pltpu.SemaphoreType.DMA((17,)),
        ],
        compiler_params=pltpu.CompilerParams(
            collective_id=0, has_side_effects=True, vmem_limit_bytes=VMEM
        ),
    )(
        queries,
        out_grad,
        attn_out,
        log_totals,
        latents,
        jnp.transpose(moe_inputs),
        jnp.transpose(moe_grad),
        expert_ids.reshape(1, tokens),
        gate_weight.reshape(weight),
        up_weight.reshape(weight),
        down_weight.reshape(weight),
    )
    qg, lg, ig, gg, ug, dg = pl.pallas_call(
        functools.partial(hand_out, 6),
        out_shape=results,
        in_specs=[anywhere] * 6,
        out_specs=(anywhere,) * 6,
        scratch_shapes=[pltpu.VMEM(r.shape, BF) for r in results]
        + [pltpu.SemaphoreType.DMA((12,))],
        compiler_params=pltpu.CompilerParams(vmem_limit_bytes=VMEM),
    )(*held)
    return (
        qg,
        lg,
        jnp.transpose(ig),
        gg.reshape((1,) + weight),
        ug.reshape((1,) + weight),
        dg.reshape((1,) + weight),
    )


def solution(mesh):
    chips = mesh.shape["ctx"] // 2
    groups = mesh.shape["exp"]
    return jax.shard_map(
        functools.partial(shards, chips, groups),
        mesh=mesh,
        in_specs=(
            P("ctx", "exp", None),
            P("ctx", "exp", None),
            P("ctx", "exp", None),
            P("exp", "ctx"),
            P("ctx", None),
            P("exp", "ctx"),
            P("exp", "ctx"),
            P("exp", None),
            P("exp", "ctx", None),
            P("exp", "ctx", None),
            P("exp", "ctx", None),
        ),
        out_specs=(
            P("ctx", "exp", None),
            P("ctx", None),
            P("exp", "ctx"),
            P("exp", "ctx", None),
            P("exp", "ctx", None),
            P("exp", "ctx", None),
        ),
        check_vma=False,
    )
```

```python
import functools
import math

import jax
import jax.numpy as jnp
from jax import lax
from jax.experimental import pallas as pl
from jax.experimental.pallas import tpu as pltpu
from jax.sharding import PartitionSpec as P

MESH = pl.DeviceIdType.MESH
VMEM = 63 * 1024 * 1024
score_scale = 192.0 ** (-0.5)
BF = jnp.bfloat16
F32 = jnp.float32

(
    K_LAT,
    K_LATF,
    K_TOK,
    K_TOKG,
    K_PAIR,
    K_SUM,
    K_SUMD,
    K_DEL,
    K_DELF,
    K_HID,
    K_HIDF,
    K_BACK,
    K_KPAIR,
    K_KSUM,
    K_KCOL,
    K_ZSUM,
    K_ZOUT,
) = range(17)
KINDS = 17
(
    L_LAT,
    L_IDS,
    L_X,
    L_XG,
    L_WG,
    L_WU,
    L_WD,
    L_Q,
    L_G,
    L_A,
    L_LOG,
    O_QG,
    O_LG,
    O_IG,
    O_GG,
    O_UG,
    O_DG,
) = range(17)


def nn(a, b):
    return jnp.dot(a, b, preferred_element_type=F32)


def nt(a, b):
    return lax.dot_general(a, b, (((1,), (1,)), ((), ())), preferred_element_type=F32)


def tn(a, b):
    return lax.dot_general(a, b, (((0,), (0,)), ((), ())), preferred_element_type=F32)


def expert_step(gate, upper, dhidden):
    sig = jax.nn.sigmoid(gate)
    active = gate * sig
    hidden = (active * upper).astype(BF)
    gate_delta = (dhidden * upper * sig * (1.0 + gate * (1.0 - sig))).astype(BF)
    up_delta = (dhidden * active).astype(BF)
    return hidden, gate_delta, up_delta


def body(
    chips,
    side,
    groups,
    q_in,
    g_in,
    a_in,
    log_in,
    lat_in,
    x_in,
    xg_in,
    ids_in,
    wg_in,
    wu_in,
    wd_in,
    qg_out,
    lg_out,
    ig_out,
    gg_out,
    ug_out,
    dg_out,
    q3,
    g3,
    a3,
    logs,
    ids,
    xt,
    xgt,
    wg,
    wu,
    wd,
    q_ref,
    g_ref,
    logs_row,
    delta_row,
    place,
    obuf,
    arr,
    pair_out,
    pair_in,
    own,
    sum_out,
    sum_in,
    dl,
    back_out,
    ret,
    lat_all,
    qacc,
    kp,
    kp_b,
    kpair_in,
    ksum_out,
    ksum_in,
    kcol_out,
    kcol_in,
    zpart,
    zsum_in,
    zfin,
    zout,
    igt,
    lgt,
    lat_own,
    gg,
    ug,
    dg,
    send_sem,
    recv_sem,
    local_sem,
):
    c = lax.axis_index("ctx")
    z = lax.axis_index("exp")
    chip = lax.div(c, 2)
    core = lax.rem(c, 2)
    sib = (chip * 2 + (1 - core), z)
    length, full = lat_in.shape
    heads = q_in.shape[1]
    rows = length * heads
    width, tokens = x_in.shape
    latent = g_in.shape[2]
    half = wg_in.shape[1] // 2
    blk = 16
    experts = groups
    owners = min(4, groups)
    spacing = groups // owners
    share = length // owners
    chunk = min(512, lat_all.shape[0])
    per = chunk // length
    last = lax.div(c, per)
    here_y = lax.div(chip, side)
    here_x = lax.rem(chip, side)

    def plane(s):
        y = lax.rem(here_y + lax.div(s, side), side)
        x = lax.rem(here_x + lax.rem(s, side), side)
        return y * side + x

    def plane_back(s):
        y = lax.rem(here_y + side - lax.div(s, side), side)
        x = lax.rem(here_x + side - lax.rem(s, side), side)
        return y * side + x

    first = here_x * (1 - core) + here_y * core
    second = here_y * (1 - core) + here_x * core

    def at(f, g):
        return (g * side + f) * (1 - core) + (f * side + g) * core

    def turned(v, s):
        return lax.rem(v + s, side)

    def spread(s):
        return groups // 2 + lax.div(s, 2) * (2 * lax.rem(s, 2) - 1)

    def ahead(s):
        return lax.rem(z + spread(s), groups)

    def behind(s):
        return lax.rem(z + groups - spread(s), groups)

    def to(src, dst, kind, si, ri, dev):
        return pltpu.make_async_remote_copy(
            src_ref=src,
            dst_ref=dst,
            send_sem=send_sem.at[kind, si],
            recv_sem=recv_sem.at[kind, ri],
            device_id=dev,
            device_id_type=MESH,
        )

    def arrived(dst, kind, ri):
        to(dst, dst, kind, 0, ri, sib).wait_recv()

    def sent(src, kind, si):
        to(src, src, kind, si, 0, sib).wait_send()

    def each(lo, hi, f):
        def step(i, carry):
            f(i)
            return carry

        lax.fori_loop(lo, hi, step, 0)

    def peer(q):
        return (2 * q + core, z)

    def line_rows(zz):
        return pl.ds(pl.multiple_of(zz * blk, blk), blk)

    def block_rows(b):
        return pl.ds(pl.multiple_of(b * length, length), length)

    def share_rows(i):
        return pl.ds(pl.multiple_of(i * share, share), share)

    def owner_z(i):
        return i * spacing + (spacing // 2) * core

    mine = line_rows(z)
    my_rows = block_rows(c)
    my_block = lat_all.at[my_rows, :]
    mine_share = lax.div(z, spacing)
    is_owner = owner_z(mine_share) == z
    other_cols = pl.ds(pl.multiple_of((1 - core) * half, half), half)
    my_cols = pl.ds(pl.multiple_of(core * half, half), half)
    barrier = pltpu.get_barrier_semaphore()

    def gather_start(block, kind):
        for s in range(1, side):
            to(block(chip), block(chip), kind, s, chip, peer(at(turned(first, s), second))).start()

    def gather_second(block, kind, f):
        held = at(f, second)
        for s in range(1, side):
            si = side * (1 + lax.rem(f - first + side, side)) + s
            to(block(held), block(held), kind, si, held, peer(at(first, turned(second, s)))).start()

    def gather_first_rest(block, kind, fkind):
        def step(s):
            q = at(turned(first, side - s), second)
            arrived(block(q), kind, q)
            gather_second(block, kind, turned(first, side - s))
            to(block(q), block(q), fkind, q, q, sib).start()

        each(1, side, step)

    def gather_second_rest(block, kind, fkind):
        def step(i):
            f = turned(first, side - lax.rem(i, side))
            q = at(f, turned(second, side - lax.div(i, side)))
            arrived(block(q), kind, q)
            to(block(q), block(q), fkind, q, q, sib).start()

        each(side, chips, step)

    def gather_pending(block, kind, fkind):
        pending.append(lambda: each(1, side, lambda s: sent(block, kind, s)))
        pending.append(
            lambda: each(
                0,
                side * (side - 1),
                lambda i: sent(
                    block, kind, side * (1 + lax.div(i, side - 1)) + 1 + lax.rem(i, side - 1)
                ),
            )
        )
        pending.append(lambda: each(0, chips, lambda q: sent(block, fkind, q)))

    def lat_block(q):
        return lat_all.at[block_rows(2 * q + core), :]

    copies = {}

    def start(src, dst, i):
        copies[i] = pltpu.make_async_copy(src, dst, local_sem.at[i])
        copies[i].start()

    def ready(*which):
        for i in which:
            copies.pop(i).wait()

    pending = []

    def load():
        ksum_out[...] = jnp.zeros_like(ksum_out)
        start(ids_in, ids, L_IDS)
        start(x_in, xt, L_X)
        start(xg_in, xgt, L_XG)
        start(lat_in, lat_own, L_LAT)
        start(wg_in, wg, L_WG)
        start(wu_in, wu, L_WU)
        start(wd_in, wd, L_WD)
        start(q_in, q3, L_Q)
        start(g_in, g3, L_G)
        start(a_in, a3, L_A)
        start(log_in, logs, L_LOG)

    def greet():
        def greet_line(s):
            pl.semaphore_signal(
                barrier, inc=1, device_id=(c, ahead(s)), device_id_type=MESH
            )

        def greet_plane(s):
            pl.semaphore_signal(barrier, inc=1, device_id=peer(plane(s)), device_id_type=MESH)

        each(1, groups, greet_line)
        each(1, chips, greet_plane)
        pl.semaphore_signal(barrier, inc=1, device_id=sib, device_id_type=MESH)

    def dispatch():
        ready(L_IDS, L_X, L_XG)
        chosen = ids[...]
        onehot = (lax.broadcasted_iota(jnp.int32, (experts, tokens), 0) == chosen).astype(F32)
        before = lax.broadcasted_iota(jnp.int32, (tokens, tokens), 0) < lax.broadcasted_iota(
            jnp.int32, (tokens, tokens), 1
        )
        earlier = nn(onehot.astype(BF), before.astype(F32).astype(BF))
        rank = jnp.sum(earlier * onehot, axis=0, keepdims=True)
        slot = chosen * blk + rank.astype(jnp.int32)
        place[...] = (
            (lax.broadcasted_iota(jnp.int32, (experts * blk, tokens), 0) == slot)
            .astype(F32)
            .astype(BF)
        )
        obuf[0, :, :width] = nt(place[...], xt[...]).astype(BF)
        obuf[1, :, :width] = nt(place[...], xgt[...]).astype(BF)
        arr[:, mine, :] = obuf[:, mine, :]

    def met():
        pl.semaphore_wait(barrier, groups + chips - 1)

    def send_tokens_of(part, kind):
        def step(s):
            zz = ahead(s)
            to(obuf.at[part, line_rows(zz), :], arr.at[part, mine, :], kind, s, z, (c, zz)).start()

        each(1, groups, step)
        pending.append(lambda: each(1, groups, lambda s: sent(obuf.at[0, mine, :], kind, s)))

    def send_inputs():
        send_tokens_of(0, K_TOK)

    def send_grads():
        send_tokens_of(1, K_TOKG)

    def send_latents():
        ready(L_LAT)
        lat_all[my_rows, :full] = lat_own[...]
        gather_start(lat_block, K_LAT)
        gather_second(lat_block, K_LAT, first)
        to(my_block, my_block, K_LATF, chip, chip, sib).start()
        gather_pending(my_block, K_LAT, K_LATF)

    def pass_latents():
        gather_first_rest(lat_block, K_LAT, K_LATF)

    def pass_latents_on():
        gather_second_rest(lat_block, K_LAT, K_LATF)

    def row_values():
        ready(L_Q, L_G, L_A, L_LOG)
        q_ref[...] = q3[...].reshape(rows, full)
        g_ref[...] = g3[...].reshape(rows, latent)
        delta = jnp.sum(
            g_ref[...].astype(F32) * a3[...].reshape(rows, latent).astype(F32),
            axis=1,
            keepdims=True,
        )
        delta = delta.astype(BF).astype(F32)
        diagonal = lax.broadcasted_iota(jnp.int32, (rows, rows), 0) == lax.broadcasted_iota(
            jnp.int32, (rows, rows), 1
        )
        delta_row[...] = jnp.sum(jnp.where(diagonal, delta, 0.0), axis=0, keepdims=True)
        spread = lax.broadcasted_iota(jnp.int32, (length, rows), 0) == (
            lax.broadcasted_iota(jnp.int32, (length, rows), 1) // heads
        )
        by_head = nn(logs[...], spread.astype(F32).astype(BF))
        of_head = lax.broadcasted_iota(jnp.int32, (heads, rows), 0) == (
            lax.broadcasted_iota(jnp.int32, (heads, rows), 1) % heads
        )
        logs_row[...] = jnp.sum(jnp.where(of_head, by_head, 0.0), axis=0, keepdims=True)

    def tokens_here_of(part, kind):
        def step(s):
            zz = behind(s)
            arrived(arr.at[part, line_rows(zz), :], kind, zz)

        each(1, groups, step)

    def project_of(j, w, part):
        pair_out[j] = nn(arr[part, :, :width], w[:, other_cols])
        to(pair_out.at[j], pair_in.at[j], K_PAIR, j, j, sib).start()
        pending.append(lambda: sent(pair_out.at[j], K_PAIR, j))

    def project_inputs():
        tokens_here_of(0, K_TOK)
        ready(L_WG, L_WU)
        project_of(0, wg, 0)
        project_of(1, wu, 0)
        own[0] = nn(arr[0, :, :width], wg[:, my_cols])
        own[1] = nn(arr[0, :, :width], wu[:, my_cols])

    def project_grads():
        tokens_here_of(1, K_TOKG)
        ready(L_WD)
        project_of(2, wd, 1)
        own[2] = nn(arr[1, :, :width], wd[:, my_cols])

    def add_pair(j):
        arrived(pair_in.at[j], K_PAIR, j)
        both = own[j] + pair_in[j]
        sum_out[:, j] = both.reshape(chips, blk, half).astype(BF)
        sum_in[chip, j] = sum_out[chip, j]

    def send_sums_of(parts, kind):
        def step(s):
            q = plane(s)
            to(sum_out.at[q, parts], sum_in.at[chip, parts], kind, s, chip, peer(q)).start()

        each(1, chips, step)
        pending.append(lambda: each(1, chips, lambda s: sent(sum_out.at[0, parts], kind, s)))

    def sums_here_of(parts, kind):
        def step(s):
            q = plane_back(s)
            arrived(sum_in.at[q, parts], kind, q)

        each(1, chips, step)

    def send_input_sums():
        add_pair(0)
        add_pair(1)
        send_sums_of(pl.ds(0, 2), K_SUM)

    def send_grad_sums():
        add_pair(2)
        send_sums_of(pl.ds(2, 1), K_SUMD)

    def latents_here():
        each(0, chips, lambda q: arrived(lat_all.at[block_rows(2 * q + 1 - core), :], K_LATF, q))

    def visit(m, carry):
        at_rows = pl.ds(pl.multiple_of(m * chunk, chunk), chunk)
        keys = lat_all[at_rows, :full]
        queries = q_ref[...]
        grads = g_ref[...]
        scores = nt(keys, queries) * score_scale
        key_pos = m * chunk + lax.broadcasted_iota(jnp.int32, (chunk, rows), 0)
        query_pos = c * length + lax.broadcasted_iota(jnp.int32, (chunk, rows), 1) // heads
        weights = jnp.where(key_pos <= query_pos, jnp.exp(scores - logs_row[...]), 0.0)
        dweights = nt(keys[:, :latent], grads)
        dscores = (weights * (dweights - delta_row[...])).astype(BF)
        weights = weights.astype(BF)
        key_part = nn(dscores, queries) * score_scale
        value_part = nn(weights, grads)
        kp[at_rows, :latent] = key_part[:, :latent] + value_part
        kp[at_rows, latent:] = key_part[:, latent:]
        kp_b[at_rows, :full] = kp[at_rows, :].astype(BF)
        qacc[...] += tn(dscores, keys)
        for i in range(per // 2):
            q = m * (per // 2) + i

            @pl.when(q < chip + core)
            def _():
                theirs = block_rows(2 * q + 1 - core)
                to(kp_b.at[theirs, :], kpair_in.at[q], K_KPAIR, q, q, sib).start()

        return carry

    def attention():
        qacc[...] = jnp.zeros_like(qacc)
        lax.fori_loop(0, last + 1, visit, 0)
        attention_end()

    def attention_some():
        qacc[...] = jnp.zeros_like(qacc)
        lax.fori_loop(0, lax.div(last + 1, 2), visit, 0)

    def attention_rest():
        lax.fori_loop(lax.div(last + 1, 2), last + 1, visit, 0)
        attention_end()

    def attention_end():
        pending.append(lambda: each(0, chip + core, lambda q: sent(kpair_in.at[0], K_KPAIR, q)))
        q3[...] = (qacc[...] * score_scale).astype(BF).reshape(length, heads, full)
        start(q3, qg_out, O_QG)

    def sums_here():
        sums_here_of(pl.ds(0, 2), K_SUM)
        sums_here_of(pl.ds(2, 1), K_SUMD)

    def experts_step():
        def total_of(j):
            total = sum_in[0, j].astype(F32)
            for q in range(1, chips):
                total = total + sum_in[q, j].astype(F32)
            return total

        hidden, gate_delta, up_delta = expert_step(total_of(0), total_of(1), total_of(2))
        dl[core, chip, 0] = hidden
        dl[core, chip, 1] = gate_delta
        dl[core, chip, 2] = up_delta

    def deltas_of(q):
        return dl.at[core, q, pl.ds(1, 2)]

    def hidden_of(q):
        return dl.at[core, q, pl.ds(0, 1)]

    def all_of(q):
        return dl.at[core, q]

    def send_blocks(block, kind, fkind):
        gather_start(block, kind)
        gather_second(block, kind, first)
        here = block(chip)
        to(here, here, fkind, chip, chip, sib).start()
        gather_pending(here, kind, fkind)

    def send_all():
        send_blocks(all_of, K_DEL, K_DELF)

    def pass_all():
        gather_first_rest(all_of, K_DEL, K_DELF)

    def pass_all_on():
        gather_second_rest(all_of, K_DEL, K_DELF)

    def all_here():
        each(0, chips, lambda q: arrived(dl.at[1 - core, q], K_DELF, q))

    def send_deltas():
        send_blocks(deltas_of, K_DEL, K_DELF)

    def pass_deltas():
        gather_first_rest(deltas_of, K_DEL, K_DELF)

    def pass_deltas_on():
        gather_second_rest(deltas_of, K_DEL, K_DELF)

    def deltas_here():
        each(0, chips, lambda q: arrived(dl.at[1 - core, q, pl.ds(1, 2)], K_DELF, q))

    def send_hidden():
        send_blocks(hidden_of, K_HID, K_HIDF)

    def pass_hidden():
        gather_first_rest(hidden_of, K_HID, K_HIDF)

    def pass_hidden_on():
        gather_second_rest(hidden_of, K_HID, K_HIDF)

    def hidden_here():
        each(0, chips, lambda q: arrived(dl.at[1 - core, q, pl.ds(0, 1)], K_HIDF, q))

    def key_pairs():
        def step(q):
            arrived(kpair_in.at[q], K_KPAIR, q)
            both = kp[block_rows(2 * q + core), :] + kpair_in[q, :, :full].astype(F32)
            ksum_out[q, :, :full] = both.astype(BF)

        each(0, chip + 1 - core, step)

        @pl.when(core == 1)
        def _():
            ksum_out[chip, :, :full] = kp[my_rows, :].astype(BF)

        def send(i):
            s, g = 1 + lax.div(i, side), lax.rem(i, side)
            f = turned(first, s)
            to(
                ksum_out.at[at(f, g)],
                ksum_in.at[first * side + g],
                K_KSUM,
                i,
                first * side + g,
                peer(at(f, second)),
            ).start()

        each(0, side * (side - 1), send)
        pending.append(
            lambda: each(0, side * (side - 1), lambda i: sent(ksum_out.at[0], K_KSUM, i))
        )

    def key_lines():
        def step(i):
            s, g = 1 + lax.div(i, side), lax.rem(i, side)
            f = turned(first, side - s)
            arrived(ksum_in.at[f * side + g], K_KSUM, f * side + g)

        each(0, side * (side - 1), step)

        def line(g):
            total = ksum_out[at(first, g), :, :full].astype(F32)
            for s in range(1, side):
                total = total + ksum_in[turned(first, s) * side + g, :, :full].astype(F32)
            return total

        def send(s):
            g = turned(second, s)
            kcol_out[s, :, :full] = line(g).astype(BF)
            to(
                kcol_out.at[s], kcol_in.at[second], K_KCOL, s, second, peer(at(first, g))
            ).start()

        each(1, side, send)
        zpart[...] = line(second)
        pending.append(lambda: each(1, side, lambda s: sent(kcol_out.at[0], K_KCOL, s)))

    def delta_of(h, j):
        return dl[h, :, j].reshape(chips * blk, half)

    def go_back():
        back = jnp.zeros((groups * blk, width), F32)
        for h in range(2):
            cols = slice(h * half, (h + 1) * half)
            back = back + nt(delta_of(h, 1), wg[:, cols]) + nt(delta_of(h, 2), wu[:, cols])
        back_out[:, :width] = back.astype(BF)

        def step(s):
            zz = ahead(s)
            to(back_out.at[line_rows(zz), :], ret.at[mine, :], K_BACK, s, z, (c, zz)).start()

        each(1, groups, step)
        ret[mine, :] = back_out[mine, :]
        pending.append(lambda: each(1, groups, lambda s: sent(back_out.at[mine, :], K_BACK, s)))

    def key_sums():
        def step(s):
            g = turned(second, s)
            arrived(kcol_in.at[g], K_KCOL, g)
            zpart[...] += kcol_in[g, :, :full].astype(F32)

        each(1, side, step)
        zfin[:, :full] = zpart[...].astype(BF)

        def send_share(i):
            @pl.when(owner_z(i) != z)
            def _():
                to(
                    zfin.at[share_rows(i), :], zsum_in.at[z], K_ZSUM, i, z, (c, owner_z(i))
                ).start()

        each(0, owners, send_share)

        def share_sent(i):
            @pl.when(owner_z(i) != z)
            def _():
                sent(zfin.at[share_rows(0), :], K_ZSUM, i)

        pending.append(lambda: each(0, owners, share_sent))

    def weight_grads():
        for h in range(2):
            cols = slice(h * half, (h + 1) * half)
            gg[:, cols] = tn(arr[0, :, :width], delta_of(h, 1)).astype(BF)
            ug[:, cols] = tn(arr[0, :, :width], delta_of(h, 2)).astype(BF)
        start(gg, gg_out, O_GG)
        start(ug, ug_out, O_UG)

    def down_grads():
        for h in range(2):
            cols = slice(h * half, (h + 1) * half)
            dg[:, cols] = tn(arr[1, :, :width], delta_of(h, 0)).astype(BF)
        start(dg, dg_out, O_DG)

    def share_sums():
        @pl.when(is_owner)
        def _():
            def shares_here(s):
                zz = ahead(s)
                arrived(zsum_in.at[zz], K_ZSUM, zz)

            each(1, groups, shares_here)
            zsum_in[z] = zfin[share_rows(mine_share), :]
            total = zsum_in[0, :, :full].astype(F32)
            for zz in range(1, groups):
                total = total + zsum_in[zz, :, :full].astype(F32)
            zout[share_rows(mine_share), :full] = total.astype(BF)

            def send_rows(s):
                zz = ahead(s)
                there = zout.at[share_rows(mine_share), :]
                to(there, there, K_ZOUT, s, mine_share, (c, zz)).start()

            each(1, groups, send_rows)

        def rows_sent():
            @pl.when(is_owner)
            def _():
                each(1, groups, lambda s: sent(zfin.at[share_rows(0), :], K_ZOUT, s))

        pending.append(rows_sent)

    def back_here():
        def step(s):
            zz = behind(s)
            arrived(ret.at[line_rows(zz), :], K_BACK, zz)

        each(1, groups, step)
        igt[...] = tn(ret[:, :width], place[...]).astype(BF)
        start(igt, ig_out, O_IG)

    def rows_here():
        def step(i):
            @pl.when(owner_z(i) != z)
            def _():
                arrived(zout.at[share_rows(i), :], K_ZOUT, i)

        each(0, owners, step)
        lgt[...] = zout[:, :full]
        start(lgt, lg_out, O_LG)

    def finish():
        for wait in pending:
            wait()
        ready(*list(copies))

    for phase in (
        load,
        greet,
        dispatch,
        row_values,
        met,
        send_inputs,
        send_latents,
        send_grads,
        pass_latents,
        pass_latents_on,
        project_inputs,
        send_input_sums,
        latents_here,
        attention_some,
        project_grads,
        send_grad_sums,
        attention_rest,
        key_pairs,
        sums_here,
        experts_step,
        send_all,
        key_lines,
        pass_all,
        key_sums,
        pass_all_on,
        all_here,
        go_back,
        weight_grads,
        down_grads,
        share_sums,
        back_here,
        rows_here,
        finish,
    ):
        phase()


def hand_out(count, *refs):
    stages, sems = refs[2 * count : 3 * count], refs[3 * count]
    ins = [pltpu.make_async_copy(refs[i], stages[i], sems.at[i]) for i in range(count)]
    outs = [
        pltpu.make_async_copy(stages[i], refs[count + i], sems.at[count + i])
        for i in range(count)
    ]
    for copy in ins:
        copy.start()
    for i in range(count):
        ins[i].wait()
        outs[i].start()
    for copy in outs:
        copy.wait()


def shards(
    chips,
    groups,
    queries,
    out_grad,
    attn_out,
    log_totals,
    latents,
    moe_inputs,
    moe_grad,
    expert_ids,
    gate_weight,
    up_weight,
    down_weight,
):
    length, heads, full = queries.shape
    latent = out_grad.shape[2]
    rows = length * heads
    tokens, width = moe_inputs.shape
    hidden = gate_weight.shape[2]
    half = hidden // 2
    blk = 16
    slots = groups * blk
    keys = length * chips * 2
    side = math.isqrt(chips)
    hbm = pl.BlockSpec(memory_space=pltpu.HBM)
    anywhere = pl.BlockSpec(memory_space=pl.ANY)
    lanes = max(chips + side, groups)
    owners = min(4, groups)
    weight = (width, hidden)
    wide = -(-width // 128) * 128
    padded = -(-full // 128) * 128
    results = (
        jax.ShapeDtypeStruct((length, heads, full), BF),
        jax.ShapeDtypeStruct((length, full), BF),
        jax.ShapeDtypeStruct((width, tokens), BF),
        jax.ShapeDtypeStruct(weight, BF),
        jax.ShapeDtypeStruct(weight, BF),
        jax.ShapeDtypeStruct(weight, BF),
    )
    held = pl.pallas_call(
        functools.partial(body, chips, side, groups),
        out_shape=results,
        in_specs=[hbm] * 11,
        out_specs=(anywhere,) * 6,
        scratch_shapes=[
            pltpu.VMEM((length, heads, full), BF),
            pltpu.VMEM((length, heads, latent), BF),
            pltpu.VMEM((length, heads, latent), BF),
            pltpu.VMEM((heads, length), BF),
            pltpu.VMEM((1, tokens), jnp.int32),
            pltpu.VMEM((width, tokens), BF),
            pltpu.VMEM((width, tokens), BF),
            pltpu.VMEM(weight, BF),
            pltpu.VMEM(weight, BF),
            pltpu.VMEM(weight, BF),
            pltpu.VMEM((rows, full), BF),
            pltpu.VMEM((rows, latent), BF),
            pltpu.VMEM((1, rows), F32),
            pltpu.VMEM((1, rows), F32),
            pltpu.VMEM((slots, tokens), BF),
            pltpu.VMEM((2, slots, wide), BF),
            pltpu.VMEM((2, slots, wide), BF),
            pltpu.VMEM((3, slots, half), F32),
            pltpu.VMEM((3, slots, half), F32),
            pltpu.VMEM((3, slots, half), F32),
            pltpu.VMEM((chips, 3, blk, half), BF),
            pltpu.VMEM((chips, 3, blk, half), BF),
            pltpu.VMEM((2, chips, 3, blk, half), BF),
            pltpu.VMEM((slots, wide), BF),
            pltpu.VMEM((slots, wide), BF),
            pltpu.VMEM((keys, padded), BF),
            pltpu.VMEM((rows, full), F32),
            pltpu.VMEM((keys, full), F32),
            pltpu.VMEM((keys, padded), BF),
            pltpu.VMEM((chips, length, padded), BF),
            pltpu.VMEM((chips, length, padded), BF),
            pltpu.VMEM((chips, length, padded), BF),
            pltpu.VMEM((side, length, padded), BF),
            pltpu.VMEM((side, length, padded), BF),
            pltpu.VMEM((length, full), F32),
            pltpu.VMEM((groups, length // owners, padded), BF),
            pltpu.VMEM((length, padded), BF),
            pltpu.VMEM((length, padded), BF),
            pltpu.VMEM((width, tokens), BF),
            pltpu.VMEM((length, full), BF),
            pltpu.VMEM((length, full), BF),
            pltpu.VMEM(weight, BF),
            pltpu.VMEM(weight, BF),
            pltpu.VMEM(weight, BF),
            pltpu.SemaphoreType.DMA((KINDS, lanes)),
            pltpu.SemaphoreType.DMA((KINDS, lanes)),
            pltpu.SemaphoreType.DMA((17,)),
        ],
        compiler_params=pltpu.CompilerParams(
            collective_id=0, has_side_effects=True, vmem_limit_bytes=VMEM
        ),
    )(
        queries,
        out_grad,
        attn_out,
        log_totals,
        latents,
        jnp.transpose(moe_inputs),
        jnp.transpose(moe_grad),
        expert_ids.reshape(1, tokens),
        gate_weight.reshape(weight),
        up_weight.reshape(weight),
        down_weight.reshape(weight),
    )
    qg, lg, ig, gg, ug, dg = pl.pallas_call(
        functools.partial(hand_out, 6),
        out_shape=results,
        in_specs=[anywhere] * 6,
        out_specs=(anywhere,) * 6,
        scratch_shapes=[pltpu.VMEM(r.shape, BF) for r in results]
        + [pltpu.SemaphoreType.DMA((12,))],
        compiler_params=pltpu.CompilerParams(vmem_limit_bytes=VMEM),
    )(*held)
    return (
        qg,
        lg,
        jnp.transpose(ig),
        gg.reshape((1,) + weight),
        ug.reshape((1,) + weight),
        dg.reshape((1,) + weight),
    )


def solution(mesh):
    chips = mesh.shape["ctx"] // 2
    groups = mesh.shape["exp"]
    return jax.shard_map(
        functools.partial(shards, chips, groups),
        mesh=mesh,
        in_specs=(
            P("ctx", "exp", None),
            P("ctx", "exp", None),
            P("ctx", "exp", None),
            P("exp", "ctx"),
            P("ctx", None),
            P("exp", "ctx"),
            P("exp", "ctx"),
            P("exp", None),
            P("exp", "ctx", None),
            P("exp", "ctx", None),
            P("exp", "ctx", None),
        ),
        out_specs=(
            P("ctx", "exp", None),
            P("ctx", None),
            P("exp", "ctx"),
            P("exp", "ctx", None),
            P("exp", "ctx", None),
            P("exp", "ctx", None),
        ),
        check_vma=False,
    )
```

```python
import functools
import math

import jax
import jax.numpy as jnp
from jax import lax
from jax.experimental import pallas as pl
from jax.experimental.pallas import tpu as pltpu
from jax.sharding import PartitionSpec as P

MESH = pl.DeviceIdType.MESH
VMEM = 63 * 1024 * 1024
score_scale = 192.0 ** (-0.5)
BF = jnp.bfloat16
F32 = jnp.float32

(
    K_LAT,
    K_LATF,
    K_TOK,
    K_TOKG,
    K_PAIR,
    K_SUM,
    K_SUMD,
    K_DEL,
    K_DELF,
    K_HID,
    K_HIDF,
    K_BACK,
    K_KPAIR,
    K_KSUM,
    K_KCOL,
    K_ZSUM,
    K_ZOUT,
) = range(17)
KINDS = 17
(
    L_LAT,
    L_IDS,
    L_X,
    L_XG,
    L_WG,
    L_WU,
    L_WD,
    L_Q,
    L_G,
    L_A,
    L_LOG,
    O_QG,
    O_LG,
    O_IG,
    O_GG,
    O_UG,
    O_DG,
) = range(17)


def nn(a, b):
    return jnp.dot(a, b, preferred_element_type=F32)


def nt(a, b):
    return lax.dot_general(a, b, (((1,), (1,)), ((), ())), preferred_element_type=F32)


def tn(a, b):
    return lax.dot_general(a, b, (((0,), (0,)), ((), ())), preferred_element_type=F32)


def expert_step(gate, upper, dhidden):
    sig = jax.nn.sigmoid(gate)
    active = gate * sig
    hidden = (active * upper).astype(BF)
    gate_delta = (dhidden * upper * sig * (1.0 + gate * (1.0 - sig))).astype(BF)
    up_delta = (dhidden * active).astype(BF)
    return hidden, gate_delta, up_delta


def body(
    chips,
    side,
    groups,
    q_in,
    g_in,
    a_in,
    log_in,
    lat_in,
    x_in,
    xg_in,
    ids_in,
    wg_in,
    wu_in,
    wd_in,
    qg_out,
    lg_out,
    ig_out,
    gg_out,
    ug_out,
    dg_out,
    q3,
    g3,
    a3,
    logs,
    ids,
    xt,
    xgt,
    wg,
    wu,
    wd,
    q_ref,
    g_ref,
    logs_row,
    delta_row,
    place,
    obuf,
    arr,
    pair_out,
    pair_in,
    own,
    sum_out,
    sum_in,
    dl,
    back_out,
    ret,
    lat_all,
    qacc,
    kp,
    kp_b,
    kpair_in,
    ksum_out,
    ksum_in,
    kcol_out,
    kcol_in,
    zpart,
    zsum_in,
    zfin,
    zout,
    igt,
    lgt,
    lat_own,
    gg,
    ug,
    dg,
    send_sem,
    recv_sem,
    local_sem,
):
    c = lax.axis_index("ctx")
    z = lax.axis_index("exp")
    chip = lax.div(c, 2)
    core = lax.rem(c, 2)
    sib = (chip * 2 + (1 - core), z)
    length, full = lat_in.shape
    heads = q_in.shape[1]
    rows = length * heads
    width, tokens = x_in.shape
    latent = g_in.shape[2]
    half = wg_in.shape[1] // 2
    blk = 16
    experts = groups
    owners = min(4, groups)
    spacing = groups // owners
    share = length // owners
    chunk = min(512, lat_all.shape[0])
    per = chunk // length
    last = lax.div(c, per)
    here_y = lax.div(chip, side)
    here_x = lax.rem(chip, side)

    def plane(s):
        y = lax.rem(here_y + lax.div(s, side), side)
        x = lax.rem(here_x + lax.rem(s, side), side)
        return y * side + x

    def plane_back(s):
        y = lax.rem(here_y + side - lax.div(s, side), side)
        x = lax.rem(here_x + side - lax.rem(s, side), side)
        return y * side + x

    first = here_x * (1 - core) + here_y * core
    second = here_y * (1 - core) + here_x * core

    def at(f, g):
        return (g * side + f) * (1 - core) + (f * side + g) * core

    def turned(v, s):
        return lax.rem(v + s, side)

    def spread(s):
        return groups // 2 + lax.div(s, 2) * (2 * lax.rem(s, 2) - 1)

    def ahead(s):
        return lax.rem(z + spread(s), groups)

    def behind(s):
        return lax.rem(z + groups - spread(s), groups)

    def to(src, dst, kind, si, ri, dev):
        return pltpu.make_async_remote_copy(
            src_ref=src,
            dst_ref=dst,
            send_sem=send_sem.at[kind, si],
            recv_sem=recv_sem.at[kind, ri],
            device_id=dev,
            device_id_type=MESH,
        )

    def arrived(dst, kind, ri):
        to(dst, dst, kind, 0, ri, sib).wait_recv()

    def sent(src, kind, si):
        to(src, src, kind, si, 0, sib).wait_send()

    def each(lo, hi, f):
        def step(i, carry):
            f(i)
            return carry

        lax.fori_loop(lo, hi, step, 0)

    def peer(q):
        return (2 * q + core, z)

    def line_rows(zz):
        return pl.ds(pl.multiple_of(zz * blk, blk), blk)

    def block_rows(b):
        return pl.ds(pl.multiple_of(b * length, length), length)

    def share_rows(i):
        return pl.ds(pl.multiple_of(i * share, share), share)

    def owner_z(i):
        return i * spacing + (spacing // 2) * core

    mine = line_rows(z)
    my_rows = block_rows(c)
    my_block = lat_all.at[my_rows, :]
    mine_share = lax.div(z, spacing)
    is_owner = owner_z(mine_share) == z
    other_cols = pl.ds(pl.multiple_of((1 - core) * half, half), half)
    my_cols = pl.ds(pl.multiple_of(core * half, half), half)
    barrier = pltpu.get_barrier_semaphore()

    def gather_start(block, kind):
        for s in range(1, side):
            to(block(chip), block(chip), kind, s, chip, peer(at(turned(first, s), second))).start()

    def gather_second(block, kind, f):
        held = at(f, second)
        for s in range(1, side):
            si = side * (1 + lax.rem(f - first + side, side)) + s
            to(block(held), block(held), kind, si, held, peer(at(first, turned(second, s)))).start()

    def gather_first_rest(block, kind, fkind):
        def step(s):
            q = at(turned(first, side - s), second)
            arrived(block(q), kind, q)
            gather_second(block, kind, turned(first, side - s))
            to(block(q), block(q), fkind, q, q, sib).start()

        each(1, side, step)

    def gather_second_rest(block, kind, fkind):
        def step(i):
            f = turned(first, side - lax.rem(i, side))
            q = at(f, turned(second, side - lax.div(i, side)))
            arrived(block(q), kind, q)
            to(block(q), block(q), fkind, q, q, sib).start()

        each(side, chips, step)

    def gather_pending(block, kind, fkind):
        pending.append(lambda: each(1, side, lambda s: sent(block, kind, s)))
        pending.append(
            lambda: each(
                0,
                side * (side - 1),
                lambda i: sent(
                    block, kind, side * (1 + lax.div(i, side - 1)) + 1 + lax.rem(i, side - 1)
                ),
            )
        )
        pending.append(lambda: each(0, chips, lambda q: sent(block, fkind, q)))

    def lat_block(q):
        return lat_all.at[block_rows(2 * q + core), :]

    copies = {}

    def start(src, dst, i):
        copies[i] = pltpu.make_async_copy(src, dst, local_sem.at[i])
        copies[i].start()

    def ready(*which):
        for i in which:
            copies.pop(i).wait()

    pending = []

    def load():
        lat_all[pl.ds(pl.multiple_of(last * chunk, chunk), chunk), :] = jnp.zeros(
            (chunk, lat_all.shape[1]), BF
        )
        ksum_out[...] = jnp.zeros_like(ksum_out)
        start(ids_in, ids, L_IDS)
        start(x_in, xt, L_X)
        start(xg_in, xgt, L_XG)
        start(lat_in, lat_own, L_LAT)
        start(wg_in, wg, L_WG)
        start(wu_in, wu, L_WU)
        start(wd_in, wd, L_WD)
        start(q_in, q3, L_Q)
        start(g_in, g3, L_G)
        start(a_in, a3, L_A)
        start(log_in, logs, L_LOG)

    def greet():
        def greet_line(s):
            pl.semaphore_signal(
                barrier, inc=1, device_id=(c, ahead(s)), device_id_type=MESH
            )

        def greet_plane(s):
            pl.semaphore_signal(barrier, inc=1, device_id=peer(plane(s)), device_id_type=MESH)

        each(1, groups, greet_line)
        each(1, chips, greet_plane)
        pl.semaphore_signal(barrier, inc=1, device_id=sib, device_id_type=MESH)

    def dispatch():
        ready(L_IDS, L_X, L_XG)
        chosen = ids[...]
        onehot = (lax.broadcasted_iota(jnp.int32, (experts, tokens), 0) == chosen).astype(F32)
        before = lax.broadcasted_iota(jnp.int32, (tokens, tokens), 0) < lax.broadcasted_iota(
            jnp.int32, (tokens, tokens), 1
        )
        earlier = nn(onehot.astype(BF), before.astype(F32).astype(BF))
        rank = jnp.sum(earlier * onehot, axis=0, keepdims=True)
        slot = chosen * blk + rank.astype(jnp.int32)
        place[...] = (
            (lax.broadcasted_iota(jnp.int32, (experts * blk, tokens), 0) == slot)
            .astype(F32)
            .astype(BF)
        )
        obuf[0, :, :width] = nt(place[...], xt[...]).astype(BF)
        obuf[1, :, :width] = nt(place[...], xgt[...]).astype(BF)
        arr[:, mine, :] = obuf[:, mine, :]

    def met():
        pl.semaphore_wait(barrier, groups + chips - 1)

    def send_tokens_of(part, kind):
        def step(s):
            zz = ahead(s)
            to(obuf.at[part, line_rows(zz), :], arr.at[part, mine, :], kind, s, z, (c, zz)).start()

        each(1, groups, step)
        pending.append(lambda: each(1, groups, lambda s: sent(obuf.at[0, mine, :], kind, s)))

    def send_inputs():
        send_tokens_of(0, K_TOK)

    def send_grads():
        send_tokens_of(1, K_TOKG)

    def to_first(b, r):
        passed = jnp.logical_and(core == 0, lax.div(b, side) < side - 1)
        return jnp.logical_or(b < r, passed)

    def latents_first(act):
        def step(s):
            r = at(turned(first, s), second)

            @pl.when(to_first(chip, r))
            def _():
                act(chip, K_LAT, s, r)

        each(1, side, step)

    def latents_second(f, act):
        held = at(f, second)

        def step(s):
            r = at(first, turned(second, s))

            @pl.when(held < r)
            def _():
                act(held, K_LAT, side * (1 + lax.rem(f - first + side, side)) + s, r)

        each(1, side, step)

    def send_block(q, kind, si, r):
        to(lat_block(q), lat_block(q), kind, si, q, peer(r)).start()

    def block_sent(q, kind, si, r):
        sent(my_block, kind, si)

    def latent_forward(q):
        to(lat_block(q), lat_block(q), K_LATF, q, q, sib).start()

    def send_latents():
        ready(L_LAT)
        lat_all[my_rows, :full] = lat_own[...]
        latents_first(send_block)
        latents_second(first, send_block)
        latent_forward(chip)
        pending.append(lambda: latents_first(block_sent))
        pending.append(lambda: latents_second(first, block_sent))
        pending.append(lambda: each(0, chip + 1, lambda q: sent(my_block, K_LATF, q)))

    def first_latents(get, act):
        def step(s):
            f = turned(first, side - s)
            q = at(f, second)

            @pl.when(to_first(q, chip))
            def _():
                get(q)
                latents_second(f, act)

        each(1, side, step)

    def pass_latents():
        def get(q):
            arrived(lat_block(q), K_LAT, q)

            @pl.when(q < chip)
            def _():
                latent_forward(q)

        first_latents(get, send_block)
        pending.append(lambda: first_latents(lambda q: None, block_sent))

    def pass_latents_on():
        def step(i):
            f = turned(first, side - lax.rem(i, side))
            q = at(f, turned(second, side - lax.div(i, side)))

            @pl.when(q < chip)
            def _():
                arrived(lat_block(q), K_LAT, q)
                latent_forward(q)

        each(side, chips, step)

    def row_values():
        ready(L_Q, L_G, L_A, L_LOG)
        q_ref[...] = q3[...].reshape(rows, full)
        g_ref[...] = g3[...].reshape(rows, latent)
        delta = jnp.sum(
            g_ref[...].astype(F32) * a3[...].reshape(rows, latent).astype(F32),
            axis=1,
            keepdims=True,
        )
        delta = delta.astype(BF).astype(F32)
        diagonal = lax.broadcasted_iota(jnp.int32, (rows, rows), 0) == lax.broadcasted_iota(
            jnp.int32, (rows, rows), 1
        )
        delta_row[...] = jnp.sum(jnp.where(diagonal, delta, 0.0), axis=0, keepdims=True)
        spread = lax.broadcasted_iota(jnp.int32, (length, rows), 0) == (
            lax.broadcasted_iota(jnp.int32, (length, rows), 1) // heads
        )
        by_head = nn(logs[...], spread.astype(F32).astype(BF))
        of_head = lax.broadcasted_iota(jnp.int32, (heads, rows), 0) == (
            lax.broadcasted_iota(jnp.int32, (heads, rows), 1) % heads
        )
        logs_row[...] = jnp.sum(jnp.where(of_head, by_head, 0.0), axis=0, keepdims=True)

    def tokens_here_of(part, kind):
        def step(s):
            zz = behind(s)
            arrived(arr.at[part, line_rows(zz), :], kind, zz)

        each(1, groups, step)

    def project_of(j, w, part):
        pair_out[j] = nn(arr[part, :, :width], w[:, other_cols])
        to(pair_out.at[j], pair_in.at[j], K_PAIR, j, j, sib).start()
        pending.append(lambda: sent(pair_out.at[j], K_PAIR, j))

    def project_inputs():
        tokens_here_of(0, K_TOK)
        ready(L_WG, L_WU)
        project_of(0, wg, 0)
        project_of(1, wu, 0)
        own[0] = nn(arr[0, :, :width], wg[:, my_cols])
        own[1] = nn(arr[0, :, :width], wu[:, my_cols])

    def project_grads():
        tokens_here_of(1, K_TOKG)
        ready(L_WD)
        project_of(2, wd, 1)
        own[2] = nn(arr[1, :, :width], wd[:, my_cols])

    def add_pair(j):
        arrived(pair_in.at[j], K_PAIR, j)
        both = own[j] + pair_in[j]
        sum_out[:, j] = both.reshape(chips, blk, half).astype(BF)
        sum_in[chip, j] = sum_out[chip, j]

    def send_sums_of(parts, kind):
        def step(s):
            q = plane(s)
            to(sum_out.at[q, parts], sum_in.at[chip, parts], kind, s, chip, peer(q)).start()

        each(1, chips, step)
        pending.append(lambda: each(1, chips, lambda s: sent(sum_out.at[0, parts], kind, s)))

    def sums_here_of(parts, kind):
        def step(s):
            q = plane_back(s)
            arrived(sum_in.at[q, parts], kind, q)

        each(1, chips, step)

    def send_input_sums():
        add_pair(0)
        add_pair(1)
        send_sums_of(pl.ds(0, 2), K_SUM)

    def send_grad_sums():
        add_pair(2)
        send_sums_of(pl.ds(2, 1), K_SUMD)

    def latents_here():
        each(
            0, chip + 1, lambda q: arrived(lat_all.at[block_rows(2 * q + 1 - core), :], K_LATF, q)
        )

    def visit(m, carry):
        at_rows = pl.ds(pl.multiple_of(m * chunk, chunk), chunk)
        keys = lat_all[at_rows, :full]
        queries = q_ref[...]
        grads = g_ref[...]
        scores = nt(keys, queries) * score_scale
        key_pos = m * chunk + lax.broadcasted_iota(jnp.int32, (chunk, rows), 0)
        query_pos = c * length + lax.broadcasted_iota(jnp.int32, (chunk, rows), 1) // heads
        weights = jnp.where(key_pos <= query_pos, jnp.exp(scores - logs_row[...]), 0.0)
        dweights = nt(keys[:, :latent], grads)
        dscores = (weights * (dweights - delta_row[...])).astype(BF)
        weights = weights.astype(BF)
        key_part = nn(dscores, queries) * score_scale
        value_part = nn(weights, grads)
        kp[at_rows, :latent] = key_part[:, :latent] + value_part
        kp[at_rows, latent:] = key_part[:, latent:]
        kp_b[at_rows, :full] = kp[at_rows, :].astype(BF)
        qacc[...] += tn(dscores, keys)
        for i in range(per // 2):
            q = m * (per // 2) + i

            @pl.when(q < chip + core)
            def _():
                theirs = block_rows(2 * q + 1 - core)
                to(kp_b.at[theirs, :], kpair_in.at[q], K_KPAIR, q, q, sib).start()

        return carry

    def attention():
        qacc[...] = jnp.zeros_like(qacc)
        lax.fori_loop(0, last + 1, visit, 0)
        attention_end()

    def attention_some():
        qacc[...] = jnp.zeros_like(qacc)
        lax.fori_loop(0, lax.div(last + 1, 2), visit, 0)

    def attention_rest():
        lax.fori_loop(lax.div(last + 1, 2), last + 1, visit, 0)
        attention_end()

    def attention_end():
        pending.append(lambda: each(0, chip + core, lambda q: sent(kpair_in.at[0], K_KPAIR, q)))
        q3[...] = (qacc[...] * score_scale).astype(BF).reshape(length, heads, full)
        start(q3, qg_out, O_QG)

    def sums_here():
        sums_here_of(pl.ds(0, 2), K_SUM)
        sums_here_of(pl.ds(2, 1), K_SUMD)

    def experts_step():
        def total_of(j):
            total = sum_in[0, j].astype(F32)
            for q in range(1, chips):
                total = total + sum_in[q, j].astype(F32)
            return total

        hidden, gate_delta, up_delta = expert_step(total_of(0), total_of(1), total_of(2))
        dl[core, chip, 0] = hidden
        dl[core, chip, 1] = gate_delta
        dl[core, chip, 2] = up_delta

    def deltas_of(q):
        return dl.at[core, q, pl.ds(1, 2)]

    def hidden_of(q):
        return dl.at[core, q, pl.ds(0, 1)]

    def all_of(q):
        return dl.at[core, q]

    def send_blocks(block, kind, fkind):
        gather_start(block, kind)
        gather_second(block, kind, first)
        here = block(chip)
        to(here, here, fkind, chip, chip, sib).start()
        gather_pending(here, kind, fkind)

    def send_all():
        send_blocks(all_of, K_DEL, K_DELF)

    def pass_all():
        gather_first_rest(all_of, K_DEL, K_DELF)

    def pass_all_on():
        gather_second_rest(all_of, K_DEL, K_DELF)

    def all_here():
        each(0, chips, lambda q: arrived(dl.at[1 - core, q], K_DELF, q))

    def send_deltas():
        send_blocks(deltas_of, K_DEL, K_DELF)

    def pass_deltas():
        gather_first_rest(deltas_of, K_DEL, K_DELF)

    def pass_deltas_on():
        gather_second_rest(deltas_of, K_DEL, K_DELF)

    def deltas_here():
        each(0, chips, lambda q: arrived(dl.at[1 - core, q, pl.ds(1, 2)], K_DELF, q))

    def send_hidden():
        send_blocks(hidden_of, K_HID, K_HIDF)

    def pass_hidden():
        gather_first_rest(hidden_of, K_HID, K_HIDF)

    def pass_hidden_on():
        gather_second_rest(hidden_of, K_HID, K_HIDF)

    def hidden_here():
        each(0, chips, lambda q: arrived(dl.at[1 - core, q, pl.ds(0, 1)], K_HIDF, q))

    def key_pairs():
        def step(q):
            arrived(kpair_in.at[q], K_KPAIR, q)
            both = kp[block_rows(2 * q + core), :] + kpair_in[q, :, :full].astype(F32)
            ksum_out[q, :, :full] = both.astype(BF)

        each(0, chip + 1 - core, step)

        @pl.when(core == 1)
        def _():
            ksum_out[chip, :, :full] = kp[my_rows, :].astype(BF)

        def send(i):
            s, g = 1 + lax.div(i, side), lax.rem(i, side)
            f = turned(first, s)
            to(
                ksum_out.at[at(f, g)],
                ksum_in.at[first * side + g],
                K_KSUM,
                i,
                first * side + g,
                peer(at(f, second)),
            ).start()

        each(0, side * (side - 1), send)
        pending.append(
            lambda: each(0, side * (side - 1), lambda i: sent(ksum_out.at[0], K_KSUM, i))
        )

    def key_lines():
        def step(i):
            s, g = 1 + lax.div(i, side), lax.rem(i, side)
            f = turned(first, side - s)
            arrived(ksum_in.at[f * side + g], K_KSUM, f * side + g)

        each(0, side * (side - 1), step)

        def line(g):
            total = ksum_out[at(first, g), :, :full].astype(F32)
            for s in range(1, side):
                total = total + ksum_in[turned(first, s) * side + g, :, :full].astype(F32)
            return total

        def send(s):
            g = turned(second, s)
            kcol_out[s, :, :full] = line(g).astype(BF)
            to(
                kcol_out.at[s], kcol_in.at[second], K_KCOL, s, second, peer(at(first, g))
            ).start()

        each(1, side, send)
        zpart[...] = line(second)
        pending.append(lambda: each(1, side, lambda s: sent(kcol_out.at[0], K_KCOL, s)))

    def delta_of(h, j):
        return dl[h, :, j].reshape(chips * blk, half)

    def go_back():
        back = jnp.zeros((groups * blk, width), F32)
        for h in range(2):
            cols = slice(h * half, (h + 1) * half)
            back = back + nt(delta_of(h, 1), wg[:, cols]) + nt(delta_of(h, 2), wu[:, cols])
        back_out[:, :width] = back.astype(BF)

        def step(s):
            zz = ahead(s)
            to(back_out.at[line_rows(zz), :], ret.at[mine, :], K_BACK, s, z, (c, zz)).start()

        each(1, groups, step)
        ret[mine, :] = back_out[mine, :]
        pending.append(lambda: each(1, groups, lambda s: sent(back_out.at[mine, :], K_BACK, s)))

    def key_sums():
        def step(s):
            g = turned(second, s)
            arrived(kcol_in.at[g], K_KCOL, g)
            zpart[...] += kcol_in[g, :, :full].astype(F32)

        each(1, side, step)
        zfin[:, :full] = zpart[...].astype(BF)

        def send_share(i):
            @pl.when(owner_z(i) != z)
            def _():
                to(
                    zfin.at[share_rows(i), :], zsum_in.at[z], K_ZSUM, i, z, (c, owner_z(i))
                ).start()

        each(0, owners, send_share)

        def share_sent(i):
            @pl.when(owner_z(i) != z)
            def _():
                sent(zfin.at[share_rows(0), :], K_ZSUM, i)

        pending.append(lambda: each(0, owners, share_sent))

    def weight_grads():
        for h in range(2):
            cols = slice(h * half, (h + 1) * half)
            gg[:, cols] = tn(arr[0, :, :width], delta_of(h, 1)).astype(BF)
            ug[:, cols] = tn(arr[0, :, :width], delta_of(h, 2)).astype(BF)
        start(gg, gg_out, O_GG)
        start(ug, ug_out, O_UG)

    def down_grads():
        for h in range(2):
            cols = slice(h * half, (h + 1) * half)
            dg[:, cols] = tn(arr[1, :, :width], delta_of(h, 0)).astype(BF)
        start(dg, dg_out, O_DG)

    def share_sums():
        @pl.when(is_owner)
        def _():
            def shares_here(s):
                zz = ahead(s)
                arrived(zsum_in.at[zz], K_ZSUM, zz)

            each(1, groups, shares_here)
            zsum_in[z] = zfin[share_rows(mine_share), :]
            total = zsum_in[0, :, :full].astype(F32)
            for zz in range(1, groups):
                total = total + zsum_in[zz, :, :full].astype(F32)
            zout[share_rows(mine_share), :full] = total.astype(BF)

            def send_rows(s):
                zz = ahead(s)
                there = zout.at[share_rows(mine_share), :]
                to(there, there, K_ZOUT, s, mine_share, (c, zz)).start()

            each(1, groups, send_rows)

        def rows_sent():
            @pl.when(is_owner)
            def _():
                each(1, groups, lambda s: sent(zfin.at[share_rows(0), :], K_ZOUT, s))

        pending.append(rows_sent)

    def back_here():
        def step(s):
            zz = behind(s)
            arrived(ret.at[line_rows(zz), :], K_BACK, zz)

        each(1, groups, step)
        igt[...] = tn(ret[:, :width], place[...]).astype(BF)
        start(igt, ig_out, O_IG)

    def rows_here():
        def step(i):
            @pl.when(owner_z(i) != z)
            def _():
                arrived(zout.at[share_rows(i), :], K_ZOUT, i)

        each(0, owners, step)
        lgt[...] = zout[:, :full]
        start(lgt, lg_out, O_LG)

    def finish():
        for wait in pending:
            wait()
        ready(*list(copies))

    for phase in (
        load,
        greet,
        dispatch,
        row_values,
        met,
        send_inputs,
        send_latents,
        send_grads,
        pass_latents,
        pass_latents_on,
        project_inputs,
        send_input_sums,
        latents_here,
        attention_some,
        project_grads,
        send_grad_sums,
        attention_rest,
        key_pairs,
        sums_here,
        experts_step,
        send_all,
        key_lines,
        pass_all,
        key_sums,
        pass_all_on,
        all_here,
        go_back,
        weight_grads,
        down_grads,
        share_sums,
        back_here,
        rows_here,
        finish,
    ):
        phase()


def hand_out(count, *refs):
    stages, sems = refs[2 * count : 3 * count], refs[3 * count]
    ins = [pltpu.make_async_copy(refs[i], stages[i], sems.at[i]) for i in range(count)]
    outs = [
        pltpu.make_async_copy(stages[i], refs[count + i], sems.at[count + i])
        for i in range(count)
    ]
    for copy in ins:
        copy.start()
    for i in range(count):
        ins[i].wait()
        outs[i].start()
    for copy in outs:
        copy.wait()


def shards(
    chips,
    groups,
    queries,
    out_grad,
    attn_out,
    log_totals,
    latents,
    moe_inputs,
    moe_grad,
    expert_ids,
    gate_weight,
    up_weight,
    down_weight,
):
    length, heads, full = queries.shape
    latent = out_grad.shape[2]
    rows = length * heads
    tokens, width = moe_inputs.shape
    hidden = gate_weight.shape[2]
    half = hidden // 2
    blk = 16
    slots = groups * blk
    keys = length * chips * 2
    side = math.isqrt(chips)
    hbm = pl.BlockSpec(memory_space=pltpu.HBM)
    anywhere = pl.BlockSpec(memory_space=pl.ANY)
    lanes = max(chips + side, groups)
    owners = min(4, groups)
    weight = (width, hidden)
    wide = -(-width // 128) * 128
    padded = -(-full // 128) * 128
    results = (
        jax.ShapeDtypeStruct((length, heads, full), BF),
        jax.ShapeDtypeStruct((length, full), BF),
        jax.ShapeDtypeStruct((width, tokens), BF),
        jax.ShapeDtypeStruct(weight, BF),
        jax.ShapeDtypeStruct(weight, BF),
        jax.ShapeDtypeStruct(weight, BF),
    )
    held = pl.pallas_call(
        functools.partial(body, chips, side, groups),
        out_shape=results,
        in_specs=[hbm] * 11,
        out_specs=(anywhere,) * 6,
        scratch_shapes=[
            pltpu.VMEM((length, heads, full), BF),
            pltpu.VMEM((length, heads, latent), BF),
            pltpu.VMEM((length, heads, latent), BF),
            pltpu.VMEM((heads, length), BF),
            pltpu.VMEM((1, tokens), jnp.int32),
            pltpu.VMEM((width, tokens), BF),
            pltpu.VMEM((width, tokens), BF),
            pltpu.VMEM(weight, BF),
            pltpu.VMEM(weight, BF),
            pltpu.VMEM(weight, BF),
            pltpu.VMEM((rows, full), BF),
            pltpu.VMEM((rows, latent), BF),
            pltpu.VMEM((1, rows), F32),
            pltpu.VMEM((1, rows), F32),
            pltpu.VMEM((slots, tokens), BF),
            pltpu.VMEM((2, slots, wide), BF),
            pltpu.VMEM((2, slots, wide), BF),
            pltpu.VMEM((3, slots, half), F32),
            pltpu.VMEM((3, slots, half), F32),
            pltpu.VMEM((3, slots, half), F32),
            pltpu.VMEM((chips, 3, blk, half), BF),
            pltpu.VMEM((chips, 3, blk, half), BF),
            pltpu.VMEM((2, chips, 3, blk, half), BF),
            pltpu.VMEM((slots, wide), BF),
            pltpu.VMEM((slots, wide), BF),
            pltpu.VMEM((keys, padded), BF),
            pltpu.VMEM((rows, full), F32),
            pltpu.VMEM((keys, full), F32),
            pltpu.VMEM((keys, padded), BF),
            pltpu.VMEM((chips, length, padded), BF),
            pltpu.VMEM((chips, length, padded), BF),
            pltpu.VMEM((chips, length, padded), BF),
            pltpu.VMEM((side, length, padded), BF),
            pltpu.VMEM((side, length, padded), BF),
            pltpu.VMEM((length, full), F32),
            pltpu.VMEM((groups, length // owners, padded), BF),
            pltpu.VMEM((length, padded), BF),
            pltpu.VMEM((length, padded), BF),
            pltpu.VMEM((width, tokens), BF),
            pltpu.VMEM((length, full), BF),
            pltpu.VMEM((length, full), BF),
            pltpu.VMEM(weight, BF),
            pltpu.VMEM(weight, BF),
            pltpu.VMEM(weight, BF),
            pltpu.SemaphoreType.DMA((KINDS, lanes)),
            pltpu.SemaphoreType.DMA((KINDS, lanes)),
            pltpu.SemaphoreType.DMA((17,)),
        ],
        compiler_params=pltpu.CompilerParams(
            collective_id=0, has_side_effects=True, vmem_limit_bytes=VMEM
        ),
    )(
        queries,
        out_grad,
        attn_out,
        log_totals,
        latents,
        jnp.transpose(moe_inputs),
        jnp.transpose(moe_grad),
        expert_ids.reshape(1, tokens),
        gate_weight.reshape(weight),
        up_weight.reshape(weight),
        down_weight.reshape(weight),
    )
    qg, lg, ig, gg, ug, dg = pl.pallas_call(
        functools.partial(hand_out, 6),
        out_shape=results,
        in_specs=[anywhere] * 6,
        out_specs=(anywhere,) * 6,
        scratch_shapes=[pltpu.VMEM(r.shape, BF) for r in results]
        + [pltpu.SemaphoreType.DMA((12,))],
        compiler_params=pltpu.CompilerParams(vmem_limit_bytes=VMEM),
    )(*held)
    return (
        qg,
        lg,
        jnp.transpose(ig),
        gg.reshape((1,) + weight),
        ug.reshape((1,) + weight),
        dg.reshape((1,) + weight),
    )


def solution(mesh):
    chips = mesh.shape["ctx"] // 2
    groups = mesh.shape["exp"]
    return jax.shard_map(
        functools.partial(shards, chips, groups),
        mesh=mesh,
        in_specs=(
            P("ctx", "exp", None),
            P("ctx", "exp", None),
            P("ctx", "exp", None),
            P("exp", "ctx"),
            P("ctx", None),
            P("exp", "ctx"),
            P("exp", "ctx"),
            P("exp", None),
            P("exp", "ctx", None),
            P("exp", "ctx", None),
            P("exp", "ctx", None),
        ),
        out_specs=(
            P("ctx", "exp", None),
            P("ctx", None),
            P("exp", "ctx"),
            P("exp", "ctx", None),
            P("exp", "ctx", None),
            P("exp", "ctx", None),
        ),
        check_vma=False,
    )
```
